256 devices in a mesh: bal: 32 (over x, z), seq: 8 (over y, core).
Axes of the slice: x: 4, y: 4, z: 8, core: 2. Of those that a mesh axis runs over, the one named last changes fastest.
Arguments:
- tokens: bfloat16 [512, 64, 5120], P('bal', 'seq'), may hold values from -6 to 6
- w_qkv: bfloat16 [5120, 24, 384], P('bal', 'seq')
- q_gain: float32 [24, 128], P('seq')
- k_gain: float32 [24, 128], P('seq')
- modulation: float32 [32, 4, 2, 5120], P('bal'), may hold values from -3 to 3
- tile_owner: int32 [512], P('bal'), may hold values from 0 to 31, as said below
- clip_dims: int32 [32, 4, 3], P('bal'), may hold values from 0 to 4, as said below
Outputs:
- attn_out: bfloat16 [512, 64, 3072], P('bal', 'seq')
The draws below stay inside these ranges and needn't reach their ends.
Inputs may be any that keep to these rules, and one draw needn't show every extreme that they name: `tile_owner`: each owner is named by exactly 16 tiles. The 16 tiles of one bal index name any owner at most 1 times, and in every draw some owner exactly 1 times. `clip_dims`: for each owner the clips' products f h w add up to 16; entries after its last clip are 0; a clip spans at most 2 tile frames, 3 tile rows and 4 tile columns and has 4 tiles or more.
All inputs are finite; a program needn't handle non-finite values.
Results may differ from the reference program's by a relative error of at most 0.006.
Values may be sent and summed in bfloat16 or wider, within the bound.
A program may use at most 128 MiB of HBM per device.

```python
import jax
import jax.numpy as jnp
import numpy as np
from jax import lax

D = 5120
HEADS = 24
HD = 128
TILE = 64
TILES_OWN = 16
MAXCLIPS = 4
TILES = 512
N_BAL = 32


def draw_w_qkv(key, part):
    key_query, key_key, key_value = jax.random.split(jax.random.fold_in(key, 13), 3)
    head_frac = jnp.arange(HEADS, dtype=jnp.float32) / max(HEADS - 1, 1)
    base_scale = D ** (-0.5)
    spread = (3.0 ** head_frac)[None, :, None] * base_scale
    query_part = jax.random.normal(key_query, (D, HEADS, HD), jnp.float32) * spread
    key_part = jax.random.normal(key_key, (D, HEADS, HD), jnp.float32) * spread
    value_part = jax.random.normal(key_value, (D, HEADS, HD), jnp.float32) * base_scale
    return jnp.concatenate([query_part, key_part, value_part], axis=2).astype(jnp.bfloat16)


def gain_table(key, salt):
    gain_key = jax.random.fold_in(key, salt)
    return jax.random.uniform(gain_key, (HEADS, HD), jnp.float32, 0.6, 1.6)


def draw_q_gain(key, part):
    return gain_table(key, 11)


def draw_k_gain(key, part):
    return gain_table(key, 12)


def draw_tile_owner(key, part):
    key_offset, key_source, key_owner, key_shuffle = jax.random.split(jax.random.fold_in(key, 21), 4)
    offsets_perm = jax.random.permutation(key_offset, N_BAL)
    source_perm = jax.random.permutation(key_source, N_BAL)
    owner_perm = jax.random.permutation(key_owner, N_BAL)
    distinct = min(N_BAL, TILES_OWN)
    offsets = offsets_perm[jnp.arange(TILES_OWN) % distinct]
    owners = owner_perm[(source_perm[:, None] + offsets[None, :]) % N_BAL]
    row_keys = jax.random.split(key_shuffle, N_BAL)
    owners = jax.vmap(lambda row_key, row_vals: jax.random.permutation(row_key, row_vals))(row_keys, owners)
    return owners.reshape(-1).astype(jnp.int32)


def draw_clip_dims(key, part):
    table = np.array([[[2, 2, 4], [0, 0, 0], [0, 0, 0], [0, 0, 0]], [[2, 2, 2], [2, 2, 2], [0, 0, 0], [0, 0, 0]], [[1, 3, 4], [1, 2, 2], [0, 0, 0], [0, 0, 0]], [[1, 2, 2], [1, 2, 2], [1, 2, 2], [1, 2, 2]]], dtype=np.int32)
    picks = jax.random.randint(jax.random.fold_in(key, 31), (N_BAL,), 0, 4)
    return jnp.asarray(table)[picks].astype(jnp.int32)


def levels(rng, extent, cuts, least, high):
    loudness, own = 1.0, jax.random.fold_in(rng, 6)
    for position, blocks in cuts:
        heights = jnp.exp(jax.random.uniform(jax.random.fold_in(own, position), (blocks,), jnp.float32, least / len(cuts), high / len(cuts)))
        loudness = loudness * jnp.repeat(heights, extent[position] // blocks).reshape([-1 if axis == position else 1 for axis in range(len(extent))])
    return loudness


def centred(own_key, dims, deviation, most, shards=(), kind=jnp.bfloat16):
    values = deviation * jax.random.normal(own_key, dims, jnp.float32)
    if shards:
        values = values * levels(own_key, dims, shards, -0.22, 0.18)
    return jnp.clip(values, -most, most).astype(kind)


def setup_inputs(seed: int = 0) -> dict:
    arg_keys = jax.random.split(jax.random.key(seed), 8)
    tokens = centred(arg_keys[0], (TILES, TILE, D), 1.0, 6.0, ((0, 32), (1, 8)))
    w_qkv = draw_w_qkv(jax.random.fold_in(arg_keys[7], 71), 0)
    q_gain = draw_q_gain(jax.random.fold_in(arg_keys[7], 71), 0)
    k_gain = draw_k_gain(jax.random.fold_in(arg_keys[7], 71), 0)
    modulation = centred(arg_keys[4], (N_BAL, MAXCLIPS, 2, D), 0.5, 3.0, ((0, 32),), jnp.float32)
    tile_owner = draw_tile_owner(jax.random.fold_in(arg_keys[7], 71), 0)
    clip_dims = draw_clip_dims(jax.random.fold_in(arg_keys[7], 71), 0)
    return dict(tokens=tokens, w_qkv=w_qkv, q_gain=q_gain, k_gain=k_gain, modulation=modulation, tile_owner=tile_owner, clip_dims=clip_dims)


eps_norm = 1e-06
score_fill = -1e+30

def tile_layout(clip_shape):
    frames_of = clip_shape[:, 0]
    rows_of = clip_shape[:, 1]
    cols_of = clip_shape[:, 2]
    clip_sizes = (frames_of * rows_of * cols_of).astype(jnp.int32)
    clip_ends = jnp.cumsum(clip_sizes).astype(jnp.int32)
    clip_starts = clip_ends - clip_sizes
    local_index = jnp.arange(TILES_OWN, dtype=jnp.int32)
    member = lax.optimization_barrier(jnp.sum((local_index[:, None] >= clip_ends[None, :]).astype(jnp.int32), axis=1)).astype(jnp.int32)
    onehot = member[:, None] == jnp.arange(clip_shape.shape[0], dtype=jnp.int32)[None, :]

    def select_clip(values):
        return lax.optimization_barrier(jnp.sum(jnp.where(onehot, values[None, :], 0), axis=1)).astype(jnp.int32)
    offset = local_index - select_clip(clip_starts)
    height = jnp.maximum(select_clip(rows_of), 1)
    width_tiles = jnp.maximum(select_clip(cols_of), 1)
    frame_index = offset // (height * width_tiles)
    row_index = offset // width_tiles % height
    column = offset % width_tiles

    def within_one(coords):
        return jnp.abs(coords[:, None] - coords[None, :]) <= 1
    tile_mask = (member[:, None] == member[None, :]) & within_one(frame_index) & within_one(row_index) & within_one(column)
    return (onehot, tile_mask)

def clip_rows(onehot, mod_table):
    picked = lax.optimization_barrier(jnp.sum(jnp.where(onehot[:, :, None, None], mod_table[None], 0.0), axis=1))
    return (picked[:, 0], picked[:, 1])

def modulate(pieces, shift_rows, scale_rows):
    values = pieces.astype(jnp.float32)
    center = lax.optimization_barrier(jnp.mean(values, axis=-1, keepdims=True))
    spread = lax.optimization_barrier(jnp.mean(jnp.square(values - center), axis=-1, keepdims=True))
    normal = (values - center) * lax.rsqrt(spread + eps_norm)
    return (normal * (1.0 + scale_rows[:, None, :]) + shift_rows[:, None, :]).astype(jnp.bfloat16)

def attend(q_block, key_rows, values, block_mask):
    scores = jnp.einsum('qhd,khd->hqk', q_block.astype(jnp.float32), key_rows.astype(jnp.float32)) * key_rows.shape[2] ** (-0.5)
    scores = jnp.where(block_mask[None], scores, score_fill)
    largest = lax.optimization_barrier(jnp.max(scores, axis=-1, keepdims=True))
    exp_scores = jnp.exp(scores - largest)
    totals = lax.optimization_barrier(jnp.sum(exp_scores, axis=-1, keepdims=True))
    weights = (exp_scores / totals).astype(jnp.bfloat16)
    return jnp.einsum('hqk,khd->qhd', weights.astype(jnp.float32), values.astype(jnp.float32))

def reference(tokens, w_qkv, q_gain, k_gain, modulation, tile_owner, clip_dims):
    owner_order = jnp.argsort(tile_owner, stable=True).astype(jnp.int32).reshape(N_BAL, TILES_OWN)
    flat_weight = w_qkv.reshape(D, -1)
    token_count = TILES_OWN * TILE

    def one_owner(inputs):
        indices, mod_table, clip_shape = inputs
        pieces = jnp.take(tokens, indices, axis=0)
        onehot, tile_mask = tile_layout(clip_shape)
        shift_rows, scale_rows = clip_rows(onehot, mod_table)
        normed = modulate(pieces, shift_rows, scale_rows).reshape(token_count, D)
        projected = jnp.dot(normed, flat_weight, preferred_element_type=jnp.float32).reshape(token_count, HEADS, 3, HD)
        query = projected[:, :, 0]
        keyed = projected[:, :, 1]
        valued = projected[:, :, 2].astype(jnp.bfloat16)
        features = HEADS * HD
        q_scale = lax.rsqrt(lax.optimization_barrier(jnp.sum(jnp.square(query), axis=(1, 2))) / features + eps_norm)
        k_scale = lax.rsqrt(lax.optimization_barrier(jnp.sum(jnp.square(keyed), axis=(1, 2))) / features + eps_norm)
        q_normed = (query * q_scale[:, None, None] * q_gain[None]).astype(jnp.bfloat16)
        k_normed = (keyed * k_scale[:, None, None] * k_gain[None]).astype(jnp.bfloat16)
        token_mask = jnp.repeat(jnp.repeat(tile_mask, TILE, axis=0), TILE, axis=1)
        block_rows = min(512, token_count)
        outputs = []
        for block_start in range(0, token_count, block_rows):
            outputs.append(attend(q_normed[block_start:block_start + block_rows], k_normed, valued, token_mask[block_start:block_start + block_rows]))
        attended = jnp.concatenate(outputs, axis=0).astype(jnp.bfloat16)
        return attended.reshape(TILES_OWN, TILE, HEADS * HD)
    owner_tiles = lax.map(one_owner, (owner_order, modulation, clip_dims))
    result = jnp.zeros((TILES, TILE, HEADS * HD), jnp.bfloat16)
    return result.at[owner_order.reshape(-1)].set(owner_tiles.reshape(TILES, TILE, HEADS * HD))
```

```python
import jax
import jax.numpy as jnp
from jax import lax
from jax.experimental import pallas as pl
from jax.experimental.pallas import tpu as pltpu
from jax.sharding import PartitionSpec as P

HEADS = 24
HD = 128
TILES_OWN = 16
NX, NZ, NY = 4, 8, 4
N_BAL = NX * NZ
N_SEQ = 2 * NY
ROWS_B = 128

eps_norm = 1e-06
score_fill = -1e30
MESH = pl.DeviceIdType.MESH


def tile_layout(clip_shape):
    frames_of = clip_shape[:, 0]
    rows_of = clip_shape[:, 1]
    cols_of = clip_shape[:, 2]
    clip_sizes = frames_of * rows_of * cols_of
    clips = jnp.arange(clip_shape.shape[0], dtype=jnp.int32)
    upto = clips[None, :] <= clips[:, None]
    clip_ends = jnp.sum(jnp.where(upto, clip_sizes[None, :], 0), axis=1)
    clip_starts = clip_ends - clip_sizes
    local_index = jnp.arange(TILES_OWN, dtype=jnp.int32)
    member = jnp.sum((local_index[:, None] >= clip_ends[None, :]).astype(jnp.int32), axis=1)
    onehot = member[:, None] == clips[None, :]

    def select_clip(values):
        return jnp.sum(jnp.where(onehot, values[None, :], 0), axis=1)

    offset = local_index - select_clip(clip_starts)
    height = jnp.maximum(select_clip(rows_of), 1)
    width_tiles = jnp.maximum(select_clip(cols_of), 1)
    frame_index = offset // (height * width_tiles)
    row_index = offset // width_tiles % height
    column = offset % width_tiles

    def within_one(coords):
        return jnp.abs(coords[:, None] - coords[None, :]) <= 1

    tile_mask = (
        (member[:, None] == member[None, :])
        & within_one(frame_index)
        & within_one(row_index)
        & within_one(column)
    )
    return (member, tile_mask)


def attend(q_block, key_rows, values, block_mask):
    scores = jnp.einsum(
        "qhd,khd->hqk", q_block, key_rows, preferred_element_type=jnp.float32
    ) * key_rows.shape[2] ** (-0.5)
    scores = jnp.where(block_mask[None], scores, score_fill)
    largest = jnp.max(scores, axis=-1, keepdims=True)
    exp_scores = jnp.exp(scores - largest)
    totals = jnp.sum(exp_scores, axis=-1, keepdims=True)
    weights = (exp_scores / totals).astype(jnp.bfloat16)
    return jnp.einsum("hqk,khd->qhd", weights, values, preferred_element_type=jnp.float32)


def project_kernel(
    slot_tile, source_of, clip_of, tok, w_in, mod, out,
    wbuf, gbuf, obuf, rbuf,
    rel_s, rel_r, z_s, z_r, x_s, x_r, xf_s, xf_r, ax_s, ax_r, axf_s, axf_r, az_s, az_r,
    y_s, y_r, yf_s, yf_r, c_s, c_r,
):
    me = lax.axis_index("bal")
    sq = lax.axis_index("seq")
    x, z = me // NZ, me % NZ
    y, core = sq // 2, sq % 2
    d_model = tok.shape[2]
    k_group = d_model // NX
    rows = w_in.shape[1]
    half_b = ROWS_B // 2
    half_a = (rows - ROWS_B) // 2

    def bal(bx, bz):
        return {"bal": (bx % NX) * NZ + bz % NZ}

    def seq(sy, sc):
        return {"seq": (sy % NY) * 2 + sc}

    z_up, z_dn = bal(x, z + 1), bal(x, z + NZ - 1)
    x_up, x_dn = bal(x + 1, z), bal(x + NX - 1, z)
    y_up, y_dn = seq(y + 1, core), seq(y + NY - 1, core)
    other = seq(y, 1 - core)

    def copy(ref, send, recv, where):
        return pltpu.make_async_remote_copy(
            src_ref=ref, dst_ref=ref, send_sem=send, recv_sem=recv,
            device_id=where, device_id_type=MESH,
        )

    started = []

    def go(ref, send, recv, where):
        c = copy(ref, send, recv, where)
        c.start()
        started.append(c)

    def arrived(ref, send, recv):
        copy(ref, send, recv, z_up).wait_recv()

    barrier = pltpu.get_barrier_semaphore()

    @pl.loop(1, N_BAL)
    def _(d):
        pl.semaphore_signal(barrier, inc=1, device_id={"bal": (me + d) % N_BAL}, device_id_type=MESH)

    @pl.loop(1, N_SEQ)
    def _(d):
        pl.semaphore_signal(barrier, inc=1, device_id={"seq": (sq + d) % N_SEQ}, device_id_type=MESH)

    for h in range(w_in.shape[0]):
        wbuf[x, z, :, h * 384 : (h + 1) * 384] = w_in[h]
    pl.semaphore_wait(barrier, N_BAL + N_SEQ - 2)

    def b_piece(bx, bz, lo=0, size=ROWS_B):
        return wbuf.at[bx % NX, bz % NZ, pl.ds(lo, size)]

    def a_piece(bx, bz, lo=0, size=rows - ROWS_B):
        return wbuf.at[bx % NX, bz % NZ, pl.ds(ROWS_B + lo, size)]

    def a_block(bz, lo=0, size=NX):
        return wbuf.at[pl.ds(lo, size), bz % NZ, pl.ds(ROWS_B, rows - ROWS_B)]

    go(b_piece(x, z), z_s.at[0, 1], z_r.at[0, 1], z_up)
    go(b_piece(x, z), z_s.at[1, 1], z_r.at[1, 1], z_dn)
    go(a_piece(x, z), ax_s.at[0], ax_r.at[0], x_up)
    go(a_piece(x, z), ax_s.at[1], ax_r.at[1], x_dn)

    rbuf[me] = tok[slot_tile[me]]

    def relay(d):
        to = (me + d) % N_BAL
        return pltpu.make_async_remote_copy(
            src_ref=obuf.at[to], dst_ref=rbuf.at[me], send_sem=rel_s.at[d], recv_sem=rel_r.at[d],
            device_id={"bal": to}, device_id_type=MESH,
        )

    @pl.loop(1, N_BAL)
    def _(d):
        to = (me + d) % N_BAL
        obuf[to] = tok[slot_tile[to]]
        relay(d).start()

    def send_x(j, bz):
        go(b_piece(x, bz), x_s.at[0, j], x_r.at[0, j], x_up)
        go(b_piece(x, bz), x_s.at[1, j], x_r.at[1, j], x_dn)

    def pass_x(j, bz):
        arrived(b_piece(x + NX - 1, bz), x_s.at[0, j], x_r.at[0, j])
        go(b_piece(x + NX - 1, bz, 0, half_b), xf_s.at[0, j], xf_r.at[0, j], x_up)
        arrived(b_piece(x + 1, bz), x_s.at[1, j], x_r.at[1, j])
        go(b_piece(x + 1, bz, half_b, half_b), xf_s.at[1, j], xf_r.at[1, j], x_dn)

    send_x(0, z)
    arrived(a_piece(x + NX - 1, z), ax_s.at[0], ax_r.at[0])
    go(a_piece(x + NX - 1, z, 0, half_a), axf_s.at[0], axf_r.at[0], x_up)
    arrived(a_piece(x + 1, z), ax_s.at[1], ax_r.at[1])
    go(a_piece(x + 1, z, half_a, half_a), axf_s.at[1], axf_r.at[1], x_dn)

    def step_z(k):
        if k < NZ // 2:
            size, lo = (ROWS_B, 0) if k < NZ // 2 - 1 else (half_b, half_b)
            arrived(b_piece(x, z + NZ - k), z_s.at[0, k], z_r.at[0, k])
            go(b_piece(x, z + NZ - k, 0, size), z_s.at[0, k + 1], z_r.at[0, k + 1], z_up)
            arrived(b_piece(x, z + k), z_s.at[1, k], z_r.at[1, k])
            go(b_piece(x, z + k, lo, size), z_s.at[1, k + 1], z_r.at[1, k + 1], z_dn)
            send_x(NZ - k, z + NZ - k)
            send_x(k, z + k)
        else:
            arrived(b_piece(x, z + k, 0, half_b), z_s.at[0, k], z_r.at[0, k])
            arrived(b_piece(x, z + k, half_b, half_b), z_s.at[1, k], z_r.at[1, k])
            send_x(k, z + k)

    def step_az(k):
        if k < NZ // 2:
            size, lo = (NX, 0) if k < NZ // 2 - 1 else (NX // 2, NX // 2)
            arrived(a_block(z + NZ - k), az_s.at[0, k], az_r.at[0, k])
            go(a_block(z + NZ - k, 0, size), az_s.at[0, k + 1], az_r.at[0, k + 1], z_up)
            arrived(a_block(z + k), az_s.at[1, k], az_r.at[1, k])
            go(a_block(z + k, lo, size), az_s.at[1, k + 1], az_r.at[1, k + 1], z_dn)
        else:
            arrived(a_block(z + k, 0, NX // 2), az_s.at[0, k], az_r.at[0, k])
            arrived(a_block(z + k, NX // 2, NX // 2), az_s.at[1, k], az_r.at[1, k])

    step_z(1)
    arrived(a_piece(x + 2, z, 0, half_a), axf_s.at[0], axf_r.at[0])
    arrived(a_piece(x + 2, z, half_a, half_a), axf_s.at[1], axf_r.at[1])
    go(a_block(z), az_s.at[0, 1], az_r.at[0, 1], z_up)
    go(a_block(z), az_s.at[1, 1], az_r.at[1, 1], z_dn)
    pass_x(0, z)
    step_z(2)
    step_z(3)
    step_az(1)
    pass_x(1, z + 1)
    pass_x(NZ - 1, z + NZ - 1)
    step_z(4)
    step_az(2)

    @pl.loop(1, N_BAL)
    def _(d):
        came = (me + N_BAL - d) % N_BAL
        pltpu.make_async_remote_copy(
            src_ref=obuf.at[me], dst_ref=rbuf.at[came], send_sem=rel_s.at[d], recv_sem=rel_r.at[d],
            device_id={"bal": came}, device_id_type=MESH,
        ).wait_recv()

    tokens_per = tok.shape[1]

    @pl.loop(0, TILES_OWN)
    def _(r):
        values = rbuf[source_of[r]].astype(jnp.float32)
        center = jnp.mean(values, axis=-1, keepdims=True)
        away = values - center
        spread = jnp.mean(away * away, axis=-1, keepdims=True)
        clip = clip_of[r]
        shift = mod[clip, 0:1, :]
        scale = mod[clip, 1:2, :]
        normed = away * lax.rsqrt(spread + eps_norm) * (1.0 + scale) + shift
        gbuf[sq, r] = normed.astype(jnp.bfloat16)

    half_t = TILES_OWN // 2

    def piece(sy, sc, lo=0, size=TILES_OWN):
        return gbuf.at[(sy % NY) * 2 + sc, pl.ds(lo, size)]

    go(piece(y, core), y_s.at[0], y_r.at[0], y_up)
    go(piece(y, core), y_s.at[1], y_r.at[1], y_dn)
    go(piece(y, core), c_s.at[0], c_r.at[0], other)

    step_az(3)
    pass_x(2, z + 2)
    pass_x(NZ - 2, z + NZ - 2)
    step_az(4)
    pass_x(3, z + 3)
    pass_x(NZ - 3, z + NZ - 3)

    arrived(piece(y + NY - 1, core), y_s.at[0], y_r.at[0])
    go(piece(y + NY - 1, core, 0, half_t), yf_s.at[0], yf_r.at[0], y_up)
    go(piece(y + NY - 1, core), c_s.at[1], c_r.at[1], other)
    arrived(piece(y + 1, core), y_s.at[1], y_r.at[1])
    go(piece(y + 1, core, half_t, half_t), yf_s.at[1], yf_r.at[1], y_dn)
    go(piece(y + 1, core), c_s.at[2], c_r.at[2], other)
    pass_x(4, z + 4)

    for j in range(NZ):
        arrived(b_piece(x + 2, z + j, 0, half_b), xf_s.at[0, j], xf_r.at[0, j])
        arrived(b_piece(x + 2, z + j, half_b, half_b), xf_s.at[1, j], xf_r.at[1, j])

    arrived(piece(y + 2, core, 0, half_t), yf_s.at[0], yf_r.at[0])
    go(piece(y + 2, core, 0, half_t), c_s.at[3], c_r.at[3], other)
    arrived(piece(y + 2, core, half_t, half_t), yf_s.at[1], yf_r.at[1])
    go(piece(y + 2, core, half_t, half_t), c_s.at[4], c_r.at[4], other)
    arrived(piece(y, 1 - core), c_s.at[0], c_r.at[0])
    arrived(piece(y + NY - 1, 1 - core), c_s.at[1], c_r.at[1])
    arrived(piece(y + 1, 1 - core), c_s.at[2], c_r.at[2])
    arrived(piece(y + 2, 1 - core, 0, half_t), c_s.at[3], c_r.at[3])
    arrived(piece(y + 2, 1 - core, half_t, half_t), c_s.at[4], c_r.at[4])

    m = N_SEQ * TILES_OWN * tokens_per
    for g in range(NX):
        @pl.loop(0, 3)
        def _(n):
            cols = pl.ds(pl.multiple_of(n * 384, 128), 384)
            left = gbuf[:, :, :, g * k_group : (g + 1) * k_group].reshape(m, k_group)
            right = wbuf[g, :, :, cols].reshape(k_group, 384)
            part = jnp.dot(left, right, preferred_element_type=jnp.float32)
            if g == 0:
                out[:, cols] = part
            else:
                out[:, cols] += part

    @pl.loop(1, N_BAL)
    def _(d):
        relay(d).wait_send()

    for c in started:
        c.wait_send()


def project(slot_tile, source_of, clip_of, tokens, w_heads, mod_table):
    tiles, per, d_model = tokens.shape
    heads, rows, width = w_heads.shape
    dma = pltpu.SemaphoreType.DMA
    vmem = pl.BlockSpec(memory_space=pltpu.VMEM)
    smem = pl.BlockSpec(memory_space=pltpu.SMEM)
    m = N_SEQ * tiles * per
    return pl.pallas_call(
        project_kernel,
        out_shape=jax.ShapeDtypeStruct((m, heads * width), jnp.float32),
        in_specs=[smem] * 3 + [vmem] * 3,
        out_specs=vmem,
        scratch_shapes=[
            pltpu.VMEM((NX, NZ, rows, heads * width), jnp.bfloat16),
            pltpu.VMEM((N_SEQ, tiles, per, d_model), jnp.bfloat16),
            pltpu.VMEM((N_BAL, per, d_model), jnp.bfloat16),
            pltpu.VMEM((N_BAL, per, d_model), jnp.bfloat16),
            dma((N_BAL,)), dma((N_BAL,)),
            dma((2, 5)), dma((2, 5)),
            dma((2, NZ)), dma((2, NZ)),
            dma((2, NZ)), dma((2, NZ)),
            dma((2,)), dma((2,)), dma((2,)), dma((2,)),
            dma((2, 5)), dma((2, 5)),
            dma((2,)), dma((2,)), dma((2,)), dma((2,)),
            dma((5,)), dma((5,)),
        ],
        compiler_params=pltpu.CompilerParams(
            collective_id=0, has_side_effects=True, vmem_limit_bytes=58 * 2**20
        ),
        cost_estimate=pl.CostEstimate(
            flops=2 * m * d_model * heads * width, bytes_accessed=8 * 2**20, transcendentals=0
        ),
        name="relay_norm_project",
    )(slot_tile, source_of, clip_of, tokens, w_heads, mod_table)


def per_device(tokens, w_qkv, q_gain, k_gain, modulation, tile_owner, clip_dims):
    me = lax.axis_index("bal")
    owned_tiles, piece_len, width_model = tokens.shape
    owners = jnp.arange(N_BAL, dtype=jnp.int32)
    tile_ids = jnp.arange(owned_tiles, dtype=jnp.int32)
    slot_tile = jnp.sum(
        jnp.where(tile_owner[None, :] == owners[:, None], tile_ids[None, :], 0), axis=1
    )
    every_owner = lax.all_gather(tile_owner, "bal", axis=0, tiled=True).reshape(N_BAL, owned_tiles)
    gives = jnp.sum((every_owner == me).astype(jnp.int32), axis=1)
    position = jnp.sum(jnp.where(owners[None, :] < owners[:, None], gives[None, :], 0), axis=1)
    source_of = jnp.sum(
        jnp.where((position[None, :] == tile_ids[:, None]) & (gives[None, :] > 0), owners[None, :], 0),
        axis=1,
    )
    member, tile_mask = tile_layout(clip_dims[0])
    projected = project(
        slot_tile, source_of, member, tokens, w_qkv.transpose(1, 0, 2), modulation[0]
    )
    per_dev_heads = q_gain.shape[0]
    total_tokens = projected.shape[0]
    projected = projected.reshape(total_tokens, per_dev_heads, 3, -1)
    query = projected[:, :, 0]
    keyed = projected[:, :, 1]
    valued = projected[:, :, 2].astype(jnp.bfloat16)
    sums_q, sums_k = lax.psum(
        (jnp.sum(jnp.square(query), axis=(1, 2)), jnp.sum(jnp.square(keyed), axis=(1, 2))), "seq"
    )
    features = HEADS * query.shape[2]
    q_normed = (
        query * lax.rsqrt(sums_q / features + eps_norm)[:, None, None] * q_gain[None]
    ).astype(jnp.bfloat16)
    k_normed = (
        keyed * lax.rsqrt(sums_k / features + eps_norm)[:, None, None] * k_gain[None]
    ).astype(jnp.bfloat16)
    token_mask = jnp.tile(
        jnp.repeat(jnp.repeat(tile_mask, piece_len, axis=0), piece_len, axis=1), (N_SEQ, N_SEQ)
    )
    block_rows = min(512, total_tokens)
    outputs = []
    for block_start in range(0, total_tokens, block_rows):
        outputs.append(
            attend(
                q_normed[block_start : block_start + block_rows],
                k_normed,
                valued,
                token_mask[block_start : block_start + block_rows],
            )
        )
    attended = jnp.concatenate(outputs, axis=0).astype(jnp.bfloat16)
    by_token_group = attended.reshape(N_SEQ, TILES_OWN * piece_len, -1)
    per_token = lax.all_to_all(by_token_group, "seq", split_axis=0, concat_axis=2, tiled=True)
    collect = (source_of[:, None] == owners[None, :]).astype(jnp.bfloat16)
    spread_back = jnp.dot(
        collect.T, per_token.reshape(TILES_OWN, -1), preferred_element_type=jnp.float32
    ).astype(jnp.bfloat16)
    spread_back = spread_back.reshape(N_BAL, 1, piece_len, -1)
    returned = lax.all_to_all(spread_back, "bal", split_axis=0, concat_axis=0, tiled=True)
    route = (tile_owner[:, None] == owners[None, :]).astype(jnp.bfloat16)
    result = jnp.dot(
        route, returned.reshape(N_BAL, -1), preferred_element_type=jnp.float32
    ).astype(jnp.bfloat16)
    return result.reshape(owned_tiles, piece_len, -1)


def solution(mesh):
    return jax.shard_map(
        per_device,
        mesh=mesh,
        in_specs=(
            P("bal", "seq", None),
            P("bal", "seq", None),
            P("seq", None),
            P("seq", None),
            P("bal", None, None, None),
            P("bal"),
            P("bal", None, None),
        ),
        out_specs=P("bal", "seq", None),
        check_vma=False,
    )
```

```python
import jax
import jax.numpy as jnp
from jax import lax
from jax.experimental import pallas as pl
from jax.experimental.pallas import tpu as pltpu
from jax.sharding import PartitionSpec as P

HEADS = 24
HD = 128
TILES_OWN = 16
NX, NZ, NY = 4, 8, 4
N_BAL = NX * NZ
N_SEQ = 2 * NY
MAXCLIPS = 4
PER = 8
GROUP = TILES_OWN * PER
LOCAL_HEADS = HEADS // N_SEQ
WIDTH = 3 * HD
ROWS_B = 128
ORDER = ("R0", "X0", "AF", "Z1", "A0", "P0", "P1", "R", "Z2", "A1", "Z3", "P2", "A2", "Z4", "P3", "A3", "Y1", "P4", "A4", "F", "Y2")

eps_norm = 1e-06
score_fill = -1e30
LOG2_E = 1.4426950408889634
MESH = pl.DeviceIdType.MESH


def kernel(
    tile_owner, clip_dims, tok, w_in, mod, q_gain, k_gain, out,
    wbuf, gbuf, obuf, rbuf, acc, row_own, row_all, place, sums, bias, qn, kn, vn, att, heads, back, came_back, place_s,
    rel_s, rel_r, z_s, z_r, x_s, x_r, xf_s, xf_r, ax_s, ax_r, axf_s, axf_r, az_s, az_r,
    y_s, y_r, yf_s, yf_r, c_s, c_r, own_s, own_r, place_sem, sum_s, sum_r, att_s, att_r, ret_s, ret_r,
):
    me = lax.axis_index("bal")
    sq = lax.axis_index("seq")
    x, z = me // NZ, me % NZ
    y, core = sq // 2, sq % 2
    d_model = tok.shape[2]
    k_group = d_model // NX
    rows = w_in.shape[1]
    half_b = ROWS_B // 2
    half_a = (rows - ROWS_B) // 2
    half_t = TILES_OWN // 2

    def bal(bx, bz):
        return {"bal": (bx % NX) * NZ + bz % NZ}

    def seq(sy, sc):
        return {"seq": (sy % NY) * 2 + sc}

    z_up, z_dn = bal(x, z + 1), bal(x, z + NZ - 1)
    x_up, x_dn = bal(x + 1, z), bal(x + NX - 1, z)
    y_up, y_dn = seq(y + 1, core), seq(y + NY - 1, core)
    other = seq(y, 1 - core)

    def move(src, dst, send, recv, where):
        return pltpu.make_async_remote_copy(
            src_ref=src, dst_ref=dst, send_sem=send, recv_sem=recv, device_id=where, device_id_type=MESH
        )

    started = []

    def go(ref, send, recv, where):
        c = move(ref, ref, send, recv, where)
        c.start()
        started.append(c)

    def arrived(ref, send, recv):
        move(ref, ref, send, recv, z_up).wait_recv()

    barrier = pltpu.get_barrier_semaphore()

    @pl.loop(1, N_BAL)
    def _(d):
        pl.semaphore_signal(barrier, inc=1, device_id={"bal": (me + d) % N_BAL}, device_id_type=MESH)

    @pl.loop(1, N_SEQ)
    def _(d):
        pl.semaphore_signal(barrier, inc=1, device_id={"seq": (sq + d) % N_SEQ}, device_id_type=MESH)

    for h in range(LOCAL_HEADS):
        wbuf[x, z, :, h * WIDTH : (h + 1) * WIDTH] = w_in[h]
    lane8 = lax.broadcasted_iota(jnp.int32, (8, 128), 1)
    owners_row = jnp.full((8, 128), -1, jnp.int32)
    for i in range(TILES_OWN):
        owners_row = jnp.where(lane8 == i, tile_owner[i], owners_row)
    row_own[...] = owners_row
    row_all[me] = owners_row

    ends, sizes = [], []
    total = 0
    for k in range(MAXCLIPS):
        f, h, w = (clip_dims[3 * k + i] for i in range(3))
        total = total + f * h * w
        ends.append(total)
        sizes.append((h, w))

    def clip_at(index):
        return sum((index >= ends[k]).astype(jnp.int32) for k in range(MAXCLIPS))

    def layout(index):
        member = clip_at(index)
        start, height, width = (jnp.zeros_like(index) for _ in range(3))
        for k in range(MAXCLIPS):
            here = member == k
            start = jnp.where(here, ends[k - 1] if k else 0, start)
            height = jnp.where(here, sizes[k][0], height)
            width = jnp.where(here, sizes[k][1], width)
        offset = index - start
        frame = (offset >= height * width).astype(jnp.int32)
        offset = offset - frame * height * width
        row = (offset >= width).astype(jnp.int32) + (offset >= 2 * width).astype(jnp.int32)
        return member, frame, row, offset - row * width

    of_query = layout(lax.broadcasted_iota(jnp.int32, (GROUP, GROUP), 0) // PER)
    of_key = layout(lax.broadcasted_iota(jnp.int32, (GROUP, GROUP), 1) // PER)
    allowed = of_query[0] == of_key[0]
    for a, b in zip(of_query[1:], of_key[1:], strict=True):
        allowed = allowed & (jnp.abs(a - b) <= 1)
    bias_tile = jnp.where(allowed, 0.0, score_fill)
    for s in range(N_SEQ):
        bias[:, s * GROUP : (s + 1) * GROUP] = bias_tile

    pl.semaphore_wait(barrier, N_BAL + N_SEQ - 2)

    def b_piece(bx, bz, lo=0, size=ROWS_B):
        return wbuf.at[bx % NX, bz % NZ, pl.ds(lo, size)]

    def a_piece(bx, bz, lo=0, size=rows - ROWS_B):
        return wbuf.at[bx % NX, bz % NZ, pl.ds(ROWS_B + lo, size)]

    def a_block(bz, lo=0, size=NX):
        return wbuf.at[pl.ds(lo, size), bz % NZ, pl.ds(ROWS_B, rows - ROWS_B)]

    def owner_row(d, to, slot):
        return move(row_own, row_all.at[slot], own_s.at[d], own_r.at[d], {"bal": to})

    def relay(d, to, slot):
        return move(obuf.at[to], rbuf.at[slot], rel_s.at[d], rel_r.at[d], {"bal": to})

    def back_relay(d, to, slot):
        return move(back.at[to], came_back.at[slot], ret_s.at[d], ret_r.at[d], {"bal": to})

    def send_x(j, bz):
        go(b_piece(x, bz), x_s.at[0, j], x_r.at[0, j], x_up)
        go(b_piece(x, bz), x_s.at[1, j], x_r.at[1, j], x_dn)

    def pass_x(j, bz):
        arrived(b_piece(x + NX - 1, bz), x_s.at[0, j], x_r.at[0, j])
        go(b_piece(x + NX - 1, bz, 0, half_b), xf_s.at[0, j], xf_r.at[0, j], x_up)
        arrived(b_piece(x + 1, bz), x_s.at[1, j], x_r.at[1, j])
        go(b_piece(x + 1, bz, half_b, half_b), xf_s.at[1, j], xf_r.at[1, j], x_dn)

    def tiles_out():
        def tile_for(owner):
            tile = 0
            for i in range(1, TILES_OWN):
                tile = jnp.where(tile_owner[i] == owner, i, tile)
            return tile

        rbuf[me] = tok[tile_for(me)]

        @pl.loop(1, N_BAL)
        def _(d):
            to = (me + d) % N_BAL
            owner_row(d, to, me).start()
            obuf[to] = tok[tile_for(to)]
            relay(d, to, me).start()

    def tiles_in():
        @pl.loop(1, N_BAL)
        def _(d):
            source = (me + N_BAL - d) % N_BAL
            move(row_own, row_all.at[source], own_s.at[d], own_r.at[d], z_up).wait_recv()

        source_id = lax.broadcasted_iota(jnp.int32, (N_BAL, 128), 0)
        lane = lax.broadcasted_iota(jnp.int32, (N_BAL, 128), 1)
        hits = (row_all[:, 0, :] == me).astype(jnp.int32)
        gives = jnp.broadcast_to(jnp.max(hits, axis=1, keepdims=True), (N_BAL, 128))
        upto = gives
        for shift in (1, 2, 4, 8, 16):
            upto = upto + jnp.where(source_id >= shift, pltpu.roll(upto, shift, 0), 0)
        position = upto - gives
        found = jnp.where((gives > 0) & (position == lane), source_id, 0)
        place[0:N_BAL] = jnp.minimum(position, TILES_OWN - 1)
        place[N_BAL : N_BAL + 8] = jnp.broadcast_to(jnp.sum(found, axis=0, keepdims=True), (8, 128))
        fetch = pltpu.make_async_copy(place, place_s, place_sem)
        fetch.start()
        fetch.wait()

        @pl.loop(1, N_BAL)
        def _(d):
            source = (me + N_BAL - d) % N_BAL
            move(obuf.at[source], rbuf.at[source], rel_s.at[d], rel_r.at[d], z_up).wait_recv()

        @pl.loop(0, TILES_OWN)
        def _(r):
            values = rbuf[place_s[N_BAL, r]].astype(jnp.float32)
            center = jnp.mean(values, axis=-1, keepdims=True)
            away = values - center
            spread = jnp.mean(away * away, axis=-1, keepdims=True)
            clip = jnp.minimum(clip_at(r), MAXCLIPS - 1)
            shift = mod[0, clip, 0:1, :]
            scale = mod[0, clip, 1:2, :]
            normed = away * lax.rsqrt(spread + eps_norm) * (1.0 + scale) + shift
            gbuf[sq, r] = normed.astype(jnp.bfloat16)

        go(piece(y, core), y_s.at[0], y_r.at[0], y_up)
        go(piece(y, core), y_s.at[1], y_r.at[1], y_dn)
        go(piece(y, core), c_s.at[0], c_r.at[0], other)

    def step_z(k):
        if k < NZ // 2:
            size, lo = (ROWS_B, 0) if k < NZ // 2 - 1 else (half_b, half_b)
            arrived(b_piece(x, z + NZ - k), z_s.at[0, k], z_r.at[0, k])
            go(b_piece(x, z + NZ - k, 0, size), z_s.at[0, k + 1], z_r.at[0, k + 1], z_up)
            arrived(b_piece(x, z + k), z_s.at[1, k], z_r.at[1, k])
            go(b_piece(x, z + k, lo, size), z_s.at[1, k + 1], z_r.at[1, k + 1], z_dn)
            send_x(NZ - k, z + NZ - k)
            send_x(k, z + k)
        else:
            arrived(b_piece(x, z + k, 0, half_b), z_s.at[0, k], z_r.at[0, k])
            arrived(b_piece(x, z + k, half_b, half_b), z_s.at[1, k], z_r.at[1, k])
            send_x(k, z + k)

    def a_forward():
        arrived(a_piece(x + NX - 1, z), ax_s.at[0], ax_r.at[0])
        go(a_piece(x + NX - 1, z, 0, half_a), axf_s.at[0], axf_r.at[0], x_up)
        arrived(a_piece(x + 1, z), ax_s.at[1], ax_r.at[1])
        go(a_piece(x + 1, z, half_a, half_a), axf_s.at[1], axf_r.at[1], x_dn)

    def step_az(k):
        if k == 0:
            arrived(a_piece(x + 2, z, 0, half_a), axf_s.at[0], axf_r.at[0])
            arrived(a_piece(x + 2, z, half_a, half_a), axf_s.at[1], axf_r.at[1])
            go(a_block(z), az_s.at[0, 1], az_r.at[0, 1], z_up)
            go(a_block(z), az_s.at[1, 1], az_r.at[1, 1], z_dn)
        elif k < NZ // 2:
            size, lo = (NX, 0) if k < NZ // 2 - 1 else (NX // 2, NX // 2)
            arrived(a_block(z + NZ - k), az_s.at[0, k], az_r.at[0, k])
            go(a_block(z + NZ - k, 0, size), az_s.at[0, k + 1], az_r.at[0, k + 1], z_up)
            arrived(a_block(z + k), az_s.at[1, k], az_r.at[1, k])
            go(a_block(z + k, lo, size), az_s.at[1, k + 1], az_r.at[1, k + 1], z_dn)
        else:
            arrived(a_block(z + k, 0, NX // 2), az_s.at[0, k], az_r.at[0, k])
            arrived(a_block(z + k, NX // 2, NX // 2), az_s.at[1, k], az_r.at[1, k])

    def step_p(j):
        pass_x(j, z + j)
        if j not in (0, NZ // 2):
            pass_x(NZ - j, z + NZ - j)

    def far_x():
        for j in range(NZ):
            arrived(b_piece(x + 2, z + j, 0, half_b), xf_s.at[0, j], xf_r.at[0, j])
            arrived(b_piece(x + 2, z + j, half_b, half_b), xf_s.at[1, j], xf_r.at[1, j])

    def piece(sy, sc, lo=0, size=TILES_OWN):
        return gbuf.at[(sy % NY) * 2 + sc, pl.ds(lo, size)]

    def near_y():
        arrived(piece(y + NY - 1, core), y_s.at[0], y_r.at[0])
        go(piece(y + NY - 1, core, 0, half_t), yf_s.at[0], yf_r.at[0], y_up)
        go(piece(y + NY - 1, core), c_s.at[1], c_r.at[1], other)
        arrived(piece(y + 1, core), y_s.at[1], y_r.at[1])
        go(piece(y + 1, core, half_t, half_t), yf_s.at[1], yf_r.at[1], y_dn)
        go(piece(y + 1, core), c_s.at[2], c_r.at[2], other)

    def far_y():
        arrived(piece(y + 2, core, 0, half_t), yf_s.at[0], yf_r.at[0])
        go(piece(y + 2, core, 0, half_t), c_s.at[3], c_r.at[3], other)
        arrived(piece(y + 2, core, half_t, half_t), yf_s.at[1], yf_r.at[1])
        go(piece(y + 2, core, half_t, half_t), c_s.at[4], c_r.at[4], other)
        arrived(piece(y, 1 - core), c_s.at[0], c_r.at[0])
        arrived(piece(y + NY - 1, 1 - core), c_s.at[1], c_r.at[1])
        arrived(piece(y + 1, 1 - core), c_s.at[2], c_r.at[2])
        arrived(piece(y + 2, 1 - core, 0, half_t), c_s.at[3], c_r.at[3])
        arrived(piece(y + 2, 1 - core, half_t, half_t), c_s.at[4], c_r.at[4])

    go(b_piece(x, z), z_s.at[0, 1], z_r.at[0, 1], z_up)
    go(b_piece(x, z), z_s.at[1, 1], z_r.at[1, 1], z_dn)
    go(a_piece(x, z), ax_s.at[0], ax_r.at[0], x_up)
    go(a_piece(x, z), ax_s.at[1], ax_r.at[1], x_dn)
    for event in ORDER:
        if event == "R0":
            tiles_out()
        elif event == "R":
            tiles_in()
        elif event == "X0":
            send_x(0, z)
        elif event == "AF":
            a_forward()
        elif event == "F":
            far_x()
        elif event == "Y1":
            near_y()
        elif event == "Y2":
            far_y()
        else:
            {"A": step_az, "Z": step_z, "P": step_p}[event[0]](int(event[1]))

    tokens_all = N_SEQ * GROUP

    def left(g):
        return gbuf[:, :, :, g * k_group : (g + 1) * k_group].reshape(tokens_all, k_group)

    for g in range(NX):
        @pl.loop(0, LOCAL_HEADS)
        def _(h, g=g):
            cols = pl.ds(pl.multiple_of(h * WIDTH, HD), 2 * HD)
            right = wbuf[g, :, :, cols].reshape(k_group, 2 * HD)
            product = jnp.dot(left(g), right, preferred_element_type=jnp.float32)
            if g == 0:
                acc[:, cols] = product
            else:
                acc[:, cols] += product

    @pl.loop(0, N_SEQ)
    def _(s):
        lines = pl.ds(pl.multiple_of(s * GROUP, GROUP), GROUP)
        for which in range(2):
            squares = sum(
                jnp.square(acc[lines, h * WIDTH + which * HD : h * WIDTH + (which + 1) * HD])
                for h in range(LOCAL_HEADS)
            )
            line = jnp.sum(squares.T, axis=0, keepdims=True)
            sums[sq, which * 8 : which * 8 + 8, lines] = jnp.broadcast_to(line, (8, GROUP))

    def sum_row(d, to, slot):
        return move(sums.at[sq], sums.at[slot], sum_s.at[d], sum_r.at[d], {"seq": to})

    for d in range(1, N_SEQ):
        sum_row(d, (sq + d) % N_SEQ, sq).start()
    for g in range(NX):
        right = jnp.concatenate(
            [wbuf[g, :, :, h * WIDTH + 2 * HD : (h + 1) * WIDTH].reshape(k_group, HD) for h in range(LOCAL_HEADS)],
            axis=1,
        )
        product = jnp.dot(left(g), right, preferred_element_type=jnp.float32)
        for h in range(LOCAL_HEADS):
            cols = slice(h * WIDTH + 2 * HD, (h + 1) * WIDTH)
            if g == 0:
                acc[:, cols] = product[:, h * HD : (h + 1) * HD]
            else:
                acc[:, cols] += product[:, h * HD : (h + 1) * HD]

    for d in range(1, N_SEQ):
        source = (sq + N_SEQ - d) % N_SEQ
        move(sums.at[source], sums.at[source], sum_s.at[d], sum_r.at[d], z_up).wait_recv()

    @pl.loop(0, N_SEQ)
    def _(s):
        lines = pl.ds(pl.multiple_of(s * GROUP, GROUP), GROUP)
        for which, gain, to in ((0, q_gain, qn), (1, k_gain, kn)):
            line = sum(sums[t, which * 8 : which * 8 + 8, lines] for t in range(N_SEQ))
            scale = lax.rsqrt(line / (HEADS * HD) + eps_norm)
            scale = jnp.broadcast_to(scale[0:1], (HD, GROUP)).T
            for h in range(LOCAL_HEADS):
                raw = acc[lines, h * WIDTH + which * HD : h * WIDTH + (which + 1) * HD]
                to[h, lines] = (raw * scale * gain[h : h + 1]).astype(jnp.bfloat16)
        for h in range(LOCAL_HEADS):
            vn[h, lines] = acc[lines, h * WIDTH + 2 * HD : (h + 1) * WIDTH].astype(jnp.bfloat16)

    def attend(s, ref, slot):
        lines = pl.ds(pl.multiple_of(s * GROUP, GROUP), GROUP)
        for h in range(LOCAL_HEADS):
            scores = lax.dot_general(
                qn[h, lines], kn[h], (((1,), (1,)), ((), ())), preferred_element_type=jnp.float32
            )
            scores = scores * (HD**-0.5 * LOG2_E) + bias[...]
            weights = jnp.exp2(scores - jnp.max(scores, axis=-1, keepdims=True))
            totals = jnp.sum(weights, axis=-1, keepdims=True)
            result = jnp.dot(
                weights.astype(jnp.bfloat16), vn[h], preferred_element_type=jnp.float32
            ) / totals
            ref[slot, :, :, h * HD : (h + 1) * HD] = result.reshape(TILES_OWN, PER, HD).astype(jnp.bfloat16)

    def head_group(d, to, slot):
        return move(att.at[to], heads.at[slot], att_s.at[d], att_r.at[d], {"seq": to})

    @pl.loop(1, N_SEQ)
    def _(d):
        to = (sq + d) % N_SEQ
        attend(to, att, to)
        head_group(d, to, sq).start()

    attend(sq, heads, sq)

    @pl.loop(1, N_SEQ)
    def _(d):
        source = (sq + N_SEQ - d) % N_SEQ
        move(att.at[source], heads.at[source], att_s.at[d], att_r.at[d], z_up).wait_recv()

    part_width = LOCAL_HEADS * HD

    def fill(ref, slot, source):
        tile = place_s[source, 0]
        for s in range(N_SEQ):
            ref[slot, :, s * part_width : (s + 1) * part_width] = heads[s, tile]

    @pl.loop(1, N_BAL)
    def _(d):
        to = (me + d) % N_BAL
        fill(back, to, to)
        back_relay(d, to, me).start()

    fill(came_back, me, me)

    @pl.loop(1, N_BAL)
    def _(d):
        source = (me + N_BAL - d) % N_BAL
        move(back.at[source], came_back.at[source], ret_s.at[d], ret_r.at[d], z_up).wait_recv()

    for i in range(TILES_OWN):
        out[i] = came_back[tile_owner[i]]

    @pl.loop(1, N_BAL)
    def _(d):
        to = (me + d) % N_BAL
        owner_row(d, to, me).wait_send()
        relay(d, to, me).wait_send()
        back_relay(d, to, me).wait_send()

    @pl.loop(1, N_SEQ)
    def _(d):
        to = (sq + d) % N_SEQ
        sum_row(d, to, sq).wait_send()
        head_group(d, to, sq).wait_send()

    for c in started:
        c.wait_send()


def per_device(tokens, w_qkv, q_gain, k_gain, modulation, tile_owner, clip_dims):
    tiles, per, d_model = tokens.shape
    rows = w_qkv.shape[0]
    dma = pltpu.SemaphoreType.DMA
    vmem = pl.BlockSpec(memory_space=pltpu.VMEM)
    smem = pl.BlockSpec(memory_space=pltpu.SMEM)
    m = N_SEQ * GROUP
    columns = LOCAL_HEADS * WIDTH
    bf16, f32, i32 = jnp.bfloat16, jnp.float32, jnp.int32
    call = pl.pallas_call(
        kernel,
        out_shape=jax.ShapeDtypeStruct((tiles, per, HEADS * HD), bf16),
        in_specs=[smem] * 2 + [vmem] * 5,
        out_specs=vmem,
        scratch_shapes=[
            pltpu.VMEM((NX, NZ, rows, columns), bf16),
            pltpu.VMEM((N_SEQ, tiles, per, d_model), bf16),
            pltpu.VMEM((N_BAL, per, d_model), bf16),
            pltpu.VMEM((N_BAL, per, d_model), bf16),
            pltpu.VMEM((m, columns), f32),
            pltpu.VMEM((8, 128), i32),
            pltpu.VMEM((N_BAL, 8, 128), i32),
            pltpu.VMEM((N_BAL + 8, 128), i32),
            pltpu.VMEM((N_SEQ, 16, m), f32),
            pltpu.VMEM((GROUP, m), f32),
            pltpu.VMEM((LOCAL_HEADS, m, HD), bf16),
            pltpu.VMEM((LOCAL_HEADS, m, HD), bf16),
            pltpu.VMEM((LOCAL_HEADS, m, HD), bf16),
            pltpu.VMEM((N_SEQ, tiles, per, LOCAL_HEADS * HD), bf16),
            pltpu.VMEM((N_SEQ, tiles, per, LOCAL_HEADS * HD), bf16),
            pltpu.VMEM((N_BAL, per, HEADS * HD), bf16),
            pltpu.VMEM((N_BAL, per, HEADS * HD), bf16),
            pltpu.SMEM((N_BAL + 8, 128), i32),
            dma((N_BAL,)), dma((N_BAL,)),
            dma((2, 5)), dma((2, 5)),
            dma((2, NZ)), dma((2, NZ)),
            dma((2, NZ)), dma((2, NZ)),
            dma((2,)), dma((2,)), dma((2,)), dma((2,)),
            dma((2, 5)), dma((2, 5)),
            dma((2,)), dma((2,)), dma((2,)), dma((2,)),
            dma((5,)), dma((5,)),
            dma((N_BAL,)), dma((N_BAL,)), dma,
            dma((N_SEQ,)), dma((N_SEQ,)),
            dma((N_SEQ,)), dma((N_SEQ,)),
            dma((N_BAL,)), dma((N_BAL,)),
        ],
        compiler_params=pltpu.CompilerParams(
            collective_id=0, has_side_effects=True, vmem_limit_bytes=58 * 2**20
        ),
        cost_estimate=pl.CostEstimate(
            flops=2 * m * d_model * columns, bytes_accessed=8 * 2**20, transcendentals=0
        ),
        name="relaid_tile_attention",
    )
    return call(
        tile_owner, clip_dims.reshape(-1), tokens, w_qkv.transpose(1, 0, 2), modulation, q_gain, k_gain
    )


def solution(mesh):
    return jax.shard_map(
        per_device,
        mesh=mesh,
        in_specs=(
            P("bal", "seq", None),
            P("bal", "seq", None),
            P("seq", None),
            P("seq", None),
            P("bal", None, None, None),
            P("bal"),
            P("bal", None, None),
        ),
        out_specs=P("bal", "seq", None),
        check_vma=False,
    )
```

```python
import jax
import jax.numpy as jnp
from jax import lax
from jax.experimental import pallas as pl
from jax.experimental.pallas import tpu as pltpu
from jax.sharding import PartitionSpec as P

HEADS = 24
HD = 128
TILES_OWN = 16
NX, NZ, NY = 4, 8, 4
N_BAL = NX * NZ
N_SEQ = 2 * NY
MAXCLIPS = 4
PER = 8
GROUP = TILES_OWN * PER
HALF = PER // 2
PAIRS = TILES_OWN // 2
LOCAL_HEADS = HEADS // N_SEQ
WIDTH = 3 * HD
ROWS_B = 128
ORDER = (
    "R0", "X0", "AF", "Z1", "A0", "P0", "P1", "Z2", "R1", "Y1", "A1", "Z3", "P2", "R2", "Z4", "A2", "P3", "A3", "Y2", "P4", "A4",
    "F1", "F2", "M1", "F", "M2",
)

eps_norm = 1e-06
score_fill = -1e30
LOG2_E = 1.4426950408889634
MESH = pl.DeviceIdType.MESH


def kernel(
    tile_owner, clip_dims, tok, w_in, mod, q_gain, k_gain, out,
    wbuf, gbuf, halves, mods, obuf, rbuf_1, rbuf_2, acc, row_own, row_all, place, sums, bias, qn, kn, vn, att, heads_1, heads_2, heads_3, back, came_1, came_2, came_3, place_s,
    rel_s, rel_r, z_s, z_r, x_s, x_r, xf_s, xf_r, ax_s, ax_r, axf_s, axf_r, az_s, az_r,
    y_s, y_r, yf_s, yf_r, c_s, c_r, own_s, own_r, place_sem, sum_s, sum_r, att_s, att_r, ret_s, ret_r,
):
    me = lax.axis_index("bal")
    sq = lax.axis_index("seq")
    x, z = me // NZ, me % NZ
    y, core = sq // 2, sq % 2
    d_model = tok.shape[2]
    k_group = d_model // NX
    rows = w_in.shape[1]
    half_b = ROWS_B // 2
    half_a = (rows - ROWS_B) // 2
    half_d = d_model // 2
    rbuf = (rbuf_1, rbuf_2)
    heads = (heads_1, heads_2, heads_3)
    came_back = (came_1, came_2, came_3)

    def bal(bx, bz):
        return {"bal": (bx % NX) * NZ + bz % NZ}

    def seq(sy, sc):
        return {"seq": (sy % NY) * 2 + sc}

    z_up, z_dn = bal(x, z + 1), bal(x, z + NZ - 1)
    x_up, x_dn = bal(x + 1, z), bal(x + NX - 1, z)
    y_up, y_dn = seq(y + 1, core), seq(y + NY - 1, core)
    other = seq(y, 1 - core)

    def move(src, dst, send, recv, where):
        return pltpu.make_async_remote_copy(
            src_ref=src, dst_ref=dst, send_sem=send, recv_sem=recv, device_id=where, device_id_type=MESH
        )

    started = []

    def go(ref, send, recv, where):
        c = move(ref, ref, send, recv, where)
        c.start()
        started.append(c)

    def arrived(ref, send, recv):
        move(ref, ref, send, recv, z_up).wait_recv()

    barrier = pltpu.get_barrier_semaphore()

    @pl.loop(1, N_BAL)
    def _(d):
        pl.semaphore_signal(barrier, inc=1, device_id={"bal": (me + d) % N_BAL}, device_id_type=MESH)

    @pl.loop(1, N_SEQ)
    def _(d):
        pl.semaphore_signal(barrier, inc=1, device_id={"seq": (sq + d) % N_SEQ}, device_id_type=MESH)

    for h in range(LOCAL_HEADS):
        wbuf[x, z, :, h * WIDTH : (h + 1) * WIDTH] = w_in[h]
    lane8 = lax.broadcasted_iota(jnp.int32, (8, 128), 1)
    owners_row = jnp.full((8, 128), -1, jnp.int32)
    for i in range(TILES_OWN):
        owners_row = jnp.where(lane8 == i, tile_owner[i], owners_row)
    row_own[...] = owners_row
    row_all[me] = owners_row

    ends, sizes = [], []
    total = 0
    for k in range(MAXCLIPS):
        f, h, w = (clip_dims[3 * k + i] for i in range(3))
        total = total + f * h * w
        ends.append(total)
        sizes.append((h, w))

    def clip_at(index):
        return sum((index >= ends[k]).astype(jnp.int32) for k in range(MAXCLIPS))

    def layout(index):
        member = clip_at(index)
        start, height, width = (jnp.zeros_like(index) for _ in range(3))
        for k in range(MAXCLIPS):
            here = member == k
            start = jnp.where(here, ends[k - 1] if k else 0, start)
            height = jnp.where(here, sizes[k][0], height)
            width = jnp.where(here, sizes[k][1], width)
        offset = index - start
        frame = (offset >= height * width).astype(jnp.int32)
        offset = offset - frame * height * width
        row = (offset >= width).astype(jnp.int32) + (offset >= 2 * width).astype(jnp.int32)
        return member, frame, row, offset - row * width

    of_query = layout(lax.broadcasted_iota(jnp.int32, (GROUP, GROUP), 0) % (GROUP // 2) // HALF)
    of_key = layout(lax.broadcasted_iota(jnp.int32, (GROUP, GROUP), 1) % (GROUP // 2) // HALF)
    allowed = of_query[0] == of_key[0]
    for a, b in zip(of_query[1:], of_key[1:], strict=True):
        allowed = allowed & (jnp.abs(a - b) <= 1)
    bias_tile = jnp.where(allowed, 0.0, score_fill)
    for s in range(N_SEQ):
        bias[:, s * GROUP : (s + 1) * GROUP] = bias_tile

    upper = lax.broadcasted_iota(jnp.int32, (8, half_d), 0) < HALF

    def interleave(a, b):
        return jnp.where(upper, a, pltpu.roll(b, HALF, 0)), jnp.where(upper, pltpu.roll(a, HALF, 0), b)

    @pl.loop(0, TILES_OWN)
    def _(i):
        values = tok[i].astype(jnp.float32)
        for t, half in enumerate(interleave(values[:, :half_d], values[:, half_d:])):
            halves[t, i] = half.astype(jnp.bfloat16)

    for k in range(MAXCLIPS):
        for which in range(2):
            line = mod[0, k, which : which + 1, :]
            mods[k, which] = jnp.where(upper, line[:, :half_d], line[:, half_d:]) + float(which)

    pl.semaphore_wait(barrier, N_BAL + N_SEQ - 2)

    def b_piece(bx, bz, lo=0, size=ROWS_B):
        return wbuf.at[bx % NX, bz % NZ, pl.ds(lo, size)]

    def a_piece(bx, bz, lo=0, size=rows - ROWS_B):
        return wbuf.at[bx % NX, bz % NZ, pl.ds(ROWS_B + lo, size)]

    def a_block(bz, lo=0, size=NX):
        return wbuf.at[pl.ds(lo, size), bz % NZ, pl.ds(ROWS_B, rows - ROWS_B)]

    def owner_row(d, to, slot):
        return move(row_own, row_all.at[slot], own_s.at[d], own_r.at[d], {"bal": to})

    def relay(t, d, to, slot):
        return move(obuf.at[t, to], rbuf[t].at[slot], rel_s.at[t, d], rel_r.at[t, d], {"bal": to})

    def back_relay(h, d, to, slot):
        return move(back.at[h, to], came_back[h].at[slot], ret_s.at[h, d], ret_r.at[h, d], {"bal": to})

    def send_x(j, bz):
        go(b_piece(x, bz), x_s.at[0, j], x_r.at[0, j], x_up)
        go(b_piece(x, bz), x_s.at[1, j], x_r.at[1, j], x_dn)

    def pass_x(j, bz):
        arrived(b_piece(x + NX - 1, bz), x_s.at[0, j], x_r.at[0, j])
        go(b_piece(x + NX - 1, bz, 0, half_b), xf_s.at[0, j], xf_r.at[0, j], x_up)
        arrived(b_piece(x + 1, bz), x_s.at[1, j], x_r.at[1, j])
        go(b_piece(x + 1, bz, half_b, half_b), xf_s.at[1, j], xf_r.at[1, j], x_dn)

    def tiles_out():
        def tile_for(owner):
            tile = 0
            for i in range(1, TILES_OWN):
                tile = jnp.where(tile_owner[i] == owner, i, tile)
            return tile

        mine = tile_for(me)
        for t in range(2):
            rbuf[t][me] = halves[t, mine]

        @pl.loop(1, N_BAL)
        def _(d):
            to = (me + d) % N_BAL
            owner_row(d, to, me).start()
            tile = tile_for(to)
            obuf[0, to] = halves[0, tile]
            relay(0, d, to, me).start()
            obuf[1, to] = halves[1, tile]

    def find_sources():
        @pl.loop(1, N_BAL)
        def _(d):
            source = (me + N_BAL - d) % N_BAL
            move(row_own, row_all.at[source], own_s.at[d], own_r.at[d], z_up).wait_recv()

        source_id = lax.broadcasted_iota(jnp.int32, (N_BAL, 128), 0)
        lane = lax.broadcasted_iota(jnp.int32, (N_BAL, 128), 1)
        hits = (row_all[:, 0, :] == me).astype(jnp.int32)
        gives = jnp.broadcast_to(jnp.max(hits, axis=1, keepdims=True), (N_BAL, 128))
        upto = gives
        for shift in (1, 2, 4, 8, 16):
            upto = upto + jnp.where(source_id >= shift, pltpu.roll(upto, shift, 0), 0)
        position = upto - gives
        found = jnp.where((gives > 0) & (position == lane), source_id, 0)
        place[0:N_BAL] = jnp.minimum(position, TILES_OWN - 1)
        place[N_BAL : N_BAL + 8] = jnp.broadcast_to(jnp.sum(found, axis=0, keepdims=True), (8, 128))
        fetch = pltpu.make_async_copy(place, place_s, place_sem)
        fetch.start()
        fetch.wait()

    def tiles_in(t):
        @pl.loop(1, N_BAL)
        def _(d):
            source = (me + N_BAL - d) % N_BAL
            move(obuf.at[t, source], rbuf[t].at[source], rel_s.at[t, d], rel_r.at[t, d], z_up).wait_recv()

        if t == 0:
            @pl.loop(1, N_BAL)
            def _(d):
                relay(1, d, (me + d) % N_BAL, me).start()

        def over_features(values):
            line = jnp.sum(values, axis=-1, keepdims=True)
            line = jnp.broadcast_to(line, (8, 128))
            return ((line + pltpu.roll(line, HALF, 0)) * (1.0 / d_model))[:, 0:1]

        def normed(r):
            values = rbuf[t][place_s[N_BAL, r]].astype(jnp.float32)
            away = values - over_features(values)
            spread = over_features(away * away)
            clip = jnp.minimum(clip_at(r), MAXCLIPS - 1)
            return away * lax.rsqrt(spread + eps_norm) * mods[clip, 1] + mods[clip, 0]

        @pl.loop(0, PAIRS)
        def _(p):
            low, high = interleave(normed(2 * p), normed(2 * p + 1))
            gbuf[sq, t, p, :, :half_d] = low.astype(jnp.bfloat16)
            gbuf[sq, t, p, :, half_d:] = high.astype(jnp.bfloat16)

        go(piece(t, y, core), y_s.at[0, t], y_r.at[0, t], y_up)
        go(piece(t, y, core), y_s.at[1, t], y_r.at[1, t], y_dn)
        go(piece(t, y, core), c_s.at[0, t], c_r.at[0, t], other)

    def step_z(k):
        if k < NZ // 2:
            size, lo = (ROWS_B, 0) if k < NZ // 2 - 1 else (half_b, half_b)
            arrived(b_piece(x, z + NZ - k), z_s.at[0, k], z_r.at[0, k])
            go(b_piece(x, z + NZ - k, 0, size), z_s.at[0, k + 1], z_r.at[0, k + 1], z_up)
            arrived(b_piece(x, z + k), z_s.at[1, k], z_r.at[1, k])
            go(b_piece(x, z + k, lo, size), z_s.at[1, k + 1], z_r.at[1, k + 1], z_dn)
            send_x(NZ - k, z + NZ - k)
            send_x(k, z + k)
        else:
            arrived(b_piece(x, z + k, 0, half_b), z_s.at[0, k], z_r.at[0, k])
            arrived(b_piece(x, z + k, half_b, half_b), z_s.at[1, k], z_r.at[1, k])
            send_x(k, z + k)

    def a_forward():
        arrived(a_piece(x + NX - 1, z), ax_s.at[0], ax_r.at[0])
        go(a_piece(x + NX - 1, z, 0, half_a), axf_s.at[0], axf_r.at[0], x_up)
        arrived(a_piece(x + 1, z), ax_s.at[1], ax_r.at[1])
        go(a_piece(x + 1, z, half_a, half_a), axf_s.at[1], axf_r.at[1], x_dn)

    def step_az(k):
        if k == 0:
            arrived(a_piece(x + 2, z, 0, half_a), axf_s.at[0], axf_r.at[0])
            arrived(a_piece(x + 2, z, half_a, half_a), axf_s.at[1], axf_r.at[1])
            go(a_block(z), az_s.at[0, 1], az_r.at[0, 1], z_up)
            go(a_block(z), az_s.at[1, 1], az_r.at[1, 1], z_dn)
        elif k < NZ // 2:
            size, lo = (NX, 0) if k < NZ // 2 - 1 else (NX // 2, NX // 2)
            arrived(a_block(z + NZ - k), az_s.at[0, k], az_r.at[0, k])
            go(a_block(z + NZ - k, 0, size), az_s.at[0, k + 1], az_r.at[0, k + 1], z_up)
            arrived(a_block(z + k), az_s.at[1, k], az_r.at[1, k])
            go(a_block(z + k, lo, size), az_s.at[1, k + 1], az_r.at[1, k + 1], z_dn)
        else:
            arrived(a_block(z + k, 0, NX // 2), az_s.at[0, k], az_r.at[0, k])
            arrived(a_block(z + k, NX // 2, NX // 2), az_s.at[1, k], az_r.at[1, k])

    def step_p(j):
        pass_x(j, z + j)
        if j not in (0, NZ // 2):
            pass_x(NZ - j, z + NZ - j)

    def far_x():
        for j in range(NZ):
            arrived(b_piece(x + 2, z + j, 0, half_b), xf_s.at[0, j], xf_r.at[0, j])
            arrived(b_piece(x + 2, z + j, half_b, half_b), xf_s.at[1, j], xf_r.at[1, j])

    half_p = PAIRS // 2

    def piece(t, sy, sc, lo=0, size=PAIRS):
        return gbuf.at[(sy % NY) * 2 + sc, t, pl.ds(lo, size)]

    def near_y(t):
        for way, (frm, to) in enumerate(((y + NY - 1, y_up), (y + 1, y_dn))):
            arrived(piece(t, frm, core), y_s.at[way, t], y_r.at[way, t])
            go(piece(t, frm, core, way * half_p, half_p), yf_s.at[way, t], yf_r.at[way, t], to)
            go(piece(t, frm, core), c_s.at[1 + way, t], c_r.at[1 + way, t], other)

    def far_y(t):
        for way in range(2):
            far = piece(t, y + 2, core, way * half_p, half_p)
            arrived(far, yf_s.at[way, t], yf_r.at[way, t])
            go(far, c_s.at[3 + way, t], c_r.at[3 + way, t], other)
        arrived(piece(t, y, 1 - core), c_s.at[0, t], c_r.at[0, t])
        for way, frm in enumerate((y + NY - 1, y + 1)):
            arrived(piece(t, frm, 1 - core), c_s.at[1 + way, t], c_r.at[1 + way, t])
            arrived(piece(t, y + 2, 1 - core, way * half_p, half_p), c_s.at[3 + way, t], c_r.at[3 + way, t])

    tokens_all = N_SEQ * GROUP

    def left(g):
        columns = pl.ds(pl.multiple_of(g * k_group, 128), k_group)
        return gbuf[:, :, :, :, columns].reshape(tokens_all, k_group)

    def project_qk(g, first):
        @pl.loop(0, LOCAL_HEADS)
        def _(h):
            cols = pl.ds(pl.multiple_of(h * WIDTH, HD), 2 * HD)
            right = wbuf[g, :, :, cols].reshape(k_group, 2 * HD)
            product = jnp.dot(left(g), right, preferred_element_type=jnp.float32)
            if first:
                acc[:, cols] = product
            else:
                acc[:, cols] += product

    def project_v(g, first):
        right = jnp.concatenate(
            [wbuf[g, :, :, h * WIDTH + 2 * HD : (h + 1) * WIDTH].reshape(k_group, HD) for h in range(LOCAL_HEADS)],
            axis=1,
        )
        product = jnp.dot(left(g), right, preferred_element_type=jnp.float32)
        for h in range(LOCAL_HEADS):
            cols = slice(h * WIDTH + 2 * HD, (h + 1) * WIDTH)
            if first:
                acc[:, cols] = product[:, h * HD : (h + 1) * HD]
            else:
                acc[:, cols] += product[:, h * HD : (h + 1) * HD]

    def project_near():
        for i, step in enumerate((0, 1, NX - 1)):
            project_qk((x + step) % NX, i == 0)

    go(b_piece(x, z), z_s.at[0, 1], z_r.at[0, 1], z_up)
    go(b_piece(x, z), z_s.at[1, 1], z_r.at[1, 1], z_dn)
    go(a_piece(x, z), ax_s.at[0], ax_r.at[0], x_up)
    go(a_piece(x, z), ax_s.at[1], ax_r.at[1], x_dn)
    for event in ORDER:
        if event == "R0":
            tiles_out()
        elif event == "R1":
            find_sources()
            tiles_in(0)
        elif event == "R2":
            tiles_in(1)
        elif event == "X0":
            send_x(0, z)
        elif event == "AF":
            a_forward()
        elif event == "F":
            far_x()
        elif event == "M1":
            project_near()
        elif event == "M2":
            project_qk((x + 2) % NX, False)
        else:
            number = int(event[1])
            if event[0] == "Y":
                near_y(number - 1)
            elif event[0] == "F":
                far_y(number - 1)
            else:
                {"A": step_az, "Z": step_z, "P": step_p}[event[0]](number)

    @pl.loop(0, N_SEQ)
    def _(s):
        lines = pl.ds(pl.multiple_of(s * GROUP, GROUP), GROUP)
        for which in range(2):
            squares = sum(
                jnp.square(acc[lines, h * WIDTH + which * HD : h * WIDTH + (which + 1) * HD])
                for h in range(LOCAL_HEADS)
            )
            line = jnp.sum(squares.T, axis=0, keepdims=True)
            sums[sq, which * 8 : which * 8 + 8, lines] = jnp.broadcast_to(line, (8, GROUP))

    def sum_row(d, to, slot):
        return move(sums.at[sq], sums.at[slot], sum_s.at[d], sum_r.at[d], {"seq": to})

    for d in range(1, N_SEQ):
        sum_row(d, (sq + d) % N_SEQ, sq).start()
    for i, step in enumerate((0, 1, NX - 1, 2)):
        project_v((x + step) % NX, i == 0)

    for d in range(1, N_SEQ):
        source = (sq + N_SEQ - d) % N_SEQ
        move(sums.at[source], sums.at[source], sum_s.at[d], sum_r.at[d], z_up).wait_recv()

    @pl.loop(0, N_SEQ)
    def _(s):
        lines = pl.ds(pl.multiple_of(s * GROUP, GROUP), GROUP)
        for which, gain, to in ((0, q_gain, qn), (1, k_gain, kn)):
            line = sum(sums[t, which * 8 : which * 8 + 8, lines] for t in range(N_SEQ))
            scale = lax.rsqrt(line / (HEADS * HD) + eps_norm)
            scale = jnp.broadcast_to(scale[0:1], (HD, GROUP)).T
            for h in range(LOCAL_HEADS):
                raw = acc[lines, h * WIDTH + which * HD : h * WIDTH + (which + 1) * HD]
                to[h, lines] = (raw * scale * gain[h : h + 1]).astype(jnp.bfloat16)
        for h in range(LOCAL_HEADS):
            vn[h, lines] = acc[lines, h * WIDTH + 2 * HD : (h + 1) * WIDTH].astype(jnp.bfloat16)

    def attend(h, s):
        lines = pl.ds(pl.multiple_of(s * GROUP, GROUP), GROUP)
        scores = lax.dot_general(
            qn[h, lines], kn[h], (((1,), (1,)), ((), ())), preferred_element_type=jnp.float32
        )
        scores = scores * (HD**-0.5 * LOG2_E) + bias[...]
        weights = jnp.exp2(scores - jnp.max(scores, axis=-1, keepdims=True))
        totals = jnp.sum(weights, axis=-1, keepdims=True)
        result = jnp.dot(
            weights.astype(jnp.bfloat16), vn[h], preferred_element_type=jnp.float32
        ) / totals
        result = result.reshape(2, PAIRS, 8, HD)
        first, second = result[0], result[1]
        top = lax.broadcasted_iota(jnp.int32, (PAIRS, 8, HD), 1) < HALF
        even = jnp.where(top, first, pltpu.roll(second, HALF, 1))
        odd = jnp.where(top, pltpu.roll(first, HALF, 1), second)
        return jnp.stack([even, odd], axis=1).reshape(TILES_OWN, PER, HD).astype(jnp.bfloat16)

    def head_group(h, d, to, slot):
        return move(att.at[h, to], heads[h].at[slot], att_s.at[h, d], att_r.at[h, d], {"seq": to})

    def attend_all(h):
        @pl.loop(1, N_SEQ)
        def _(d):
            to = (sq + d) % N_SEQ
            att[h, to] = attend(h, to)
            head_group(h, d, to, sq).start()

        heads[h][sq] = attend(h, sq)

    def send_back(h):
        @pl.loop(1, N_SEQ)
        def _(d):
            source = (sq + N_SEQ - d) % N_SEQ
            move(att.at[h, source], heads[h].at[source], att_s.at[h, d], att_r.at[h, d], z_up).wait_recv()

        @pl.loop(1, N_BAL)
        def _(d):
            to = (me + d) % N_BAL
            tile = place_s[to, 0]
            for s in range(N_SEQ):
                back[h, to, :, s * HD : (s + 1) * HD] = heads[h][s, tile]
            back_relay(h, d, to, me).start()

        tile = place_s[me, 0]
        for s in range(N_SEQ):
            came_back[h][me, :, s * HD : (s + 1) * HD] = heads[h][s, tile]

    for h in range(LOCAL_HEADS):
        attend_all(h)
        if h:
            send_back(h - 1)
    send_back(LOCAL_HEADS - 1)

    for h in range(LOCAL_HEADS):
        @pl.loop(1, N_BAL)
        def _(d, h=h):
            source = (me + N_BAL - d) % N_BAL
            move(back.at[h, source], came_back[h].at[source], ret_s.at[h, d], ret_r.at[h, d], z_up).wait_recv()

        for i in range(TILES_OWN):
            tile = came_back[h][tile_owner[i]]
            for s in range(N_SEQ):
                column = (s * LOCAL_HEADS + h) * HD
                out[i, :, column : column + HD] = tile[:, s * HD : (s + 1) * HD]

    @pl.loop(1, N_BAL)
    def _(d):
        to = (me + d) % N_BAL
        owner_row(d, to, me).wait_send()
        relay(0, d, to, me).wait_send()
        relay(1, d, to, me).wait_send()
        for h in range(LOCAL_HEADS):
            back_relay(h, d, to, me).wait_send()

    @pl.loop(1, N_SEQ)
    def _(d):
        to = (sq + d) % N_SEQ
        sum_row(d, to, sq).wait_send()
        for h in range(LOCAL_HEADS):
            head_group(h, d, to, sq).wait_send()

    for c in started:
        c.wait_send()


def per_device(tokens, w_qkv, q_gain, k_gain, modulation, tile_owner, clip_dims):
    tiles, per, d_model = tokens.shape
    rows = w_qkv.shape[0]
    dma = pltpu.SemaphoreType.DMA
    vmem = pl.BlockSpec(memory_space=pltpu.VMEM)
    smem = pl.BlockSpec(memory_space=pltpu.SMEM)
    m = N_SEQ * GROUP
    columns = LOCAL_HEADS * WIDTH
    bf16, f32, i32 = jnp.bfloat16, jnp.float32, jnp.int32
    call = pl.pallas_call(
        kernel,
        out_shape=jax.ShapeDtypeStruct((tiles, per, HEADS * HD), bf16),
        in_specs=[smem] * 2 + [vmem] * 5,
        out_specs=vmem,
        scratch_shapes=[
            pltpu.VMEM((NX, NZ, rows, columns), bf16),
            pltpu.VMEM((N_SEQ, 2, PAIRS, 8, d_model), bf16),
            pltpu.VMEM((2, tiles, 8, d_model // 2), bf16),
            pltpu.VMEM((MAXCLIPS, 2, 8, d_model // 2), f32),
            pltpu.VMEM((2, N_BAL, 8, d_model // 2), bf16),
            pltpu.VMEM((N_BAL, 8, d_model // 2), bf16),
            pltpu.VMEM((N_BAL, 8, d_model // 2), bf16),
            pltpu.VMEM((m, columns), f32),
            pltpu.VMEM((8, 128), i32),
            pltpu.VMEM((N_BAL, 8, 128), i32),
            pltpu.VMEM((N_BAL + 8, 128), i32),
            pltpu.VMEM((N_SEQ, 16, m), f32),
            pltpu.VMEM((GROUP, m), f32),
            pltpu.VMEM((LOCAL_HEADS, m, HD), bf16),
            pltpu.VMEM((LOCAL_HEADS, m, HD), bf16),
            pltpu.VMEM((LOCAL_HEADS, m, HD), bf16),
            pltpu.VMEM((LOCAL_HEADS, N_SEQ, tiles, per, HD), bf16),
            *[pltpu.VMEM((N_SEQ, tiles, per, HD), bf16)] * LOCAL_HEADS,
            pltpu.VMEM((LOCAL_HEADS, N_BAL, per, N_SEQ * HD), bf16),
            *[pltpu.VMEM((N_BAL, per, N_SEQ * HD), bf16)] * LOCAL_HEADS,
            pltpu.SMEM((N_BAL + 8, 128), i32),
            dma((2, N_BAL)), dma((2, N_BAL)),
            dma((2, 5)), dma((2, 5)),
            dma((2, NZ)), dma((2, NZ)),
            dma((2, NZ)), dma((2, NZ)),
            dma((2,)), dma((2,)), dma((2,)), dma((2,)),
            dma((2, 5)), dma((2, 5)),
            dma((2, 2)), dma((2, 2)), dma((2, 2)), dma((2, 2)),
            dma((5, 2)), dma((5, 2)),
            dma((N_BAL,)), dma((N_BAL,)), dma,
            dma((N_SEQ,)), dma((N_SEQ,)),
            dma((LOCAL_HEADS, N_SEQ)), dma((LOCAL_HEADS, N_SEQ)),
            dma((LOCAL_HEADS, N_BAL)), dma((LOCAL_HEADS, N_BAL)),
        ],
        compiler_params=pltpu.CompilerParams(
            collective_id=0, has_side_effects=True, vmem_limit_bytes=58 * 2**20
        ),
        cost_estimate=pl.CostEstimate(
            flops=2 * m * d_model * columns, bytes_accessed=8 * 2**20, transcendentals=0
        ),
        name="relaid_tile_attention",
    )
    return call(
        tile_owner, clip_dims.reshape(-1), tokens, w_qkv.transpose(1, 0, 2), modulation, q_gain, k_gain
    )


def solution(mesh):
    return jax.shard_map(
        per_device,
        mesh=mesh,
        in_specs=(
            P("bal", "seq", None),
            P("bal", "seq", None),
            P("seq", None),
            P("seq", None),
            P("bal", None, None, None),
            P("bal"),
            P("bal", None, None),
        ),
        out_specs=P("bal", "seq", None),
        check_vma=False,
    )
```

```python
import jax
import jax.numpy as jnp
from jax import lax
from jax.experimental import pallas as pl
from jax.experimental.pallas import tpu as pltpu
from jax.sharding import PartitionSpec as P

HEADS = 24
HD = 128
TILES_OWN = 16
NX, NZ, NY = 4, 8, 4
N_BAL = NX * NZ
N_SEQ = 2 * NY
MAXCLIPS = 4
PER = 8
GROUP = TILES_OWN * PER
HALF = PER // 2
PAIRS = TILES_OWN // 2
LOCAL_HEADS = HEADS // N_SEQ
WIDTH = 3 * HD
ROWS_B = 128
ORDER = (
    "R0", "X0", "AF", "Z1", "A0", "P0", "P1", "Z2", "R1", "Y1", "A1", "Z3", "P2", "R2", "Z4", "A2", "P3", "A3", "Y2", "P4", "A4",
    "F1", "F2", "M1", "F", "M2",
)

eps_norm = 1e-06
score_fill = -1e30
LOG2_E = 1.4426950408889634
MESH = pl.DeviceIdType.MESH


def kernel(
    tile_owner, clip_dims, tok, w_in, mod, q_gain, k_gain, out,
    wbuf, gbuf, halves, mods, obuf, rbuf_1, rbuf_2, acc, row_own, row_all, place, sums, bias, qn, kn, vn, att, heads_1, heads_2, heads_3, back, came_1, came_2, came_3, place_s,
    rel_s, rel_r, z_s, z_r, x_s, x_r, xf_s, xf_r, ax_s, ax_r, axf_s, axf_r, az_s, az_r,
    y_s, y_r, yf_s, yf_r, c_s, c_r, own_s, own_r, place_sem, sum_s, sum_r, att_s, att_r, ret_s, ret_r,
):
    me = lax.axis_index("bal")
    sq = lax.axis_index("seq")
    x, z = me // NZ, me % NZ
    y, core = sq // 2, sq % 2
    d_model = tok.shape[2]
    k_group = d_model // NX
    rows = w_in.shape[1]
    half_b = ROWS_B // 2
    half_a = (rows - ROWS_B) // 2
    half_d = d_model // 2
    rbuf = (rbuf_1, rbuf_2)
    heads = (heads_1, heads_2, heads_3)
    came_back = (came_1, came_2, came_3)

    def bal(bx, bz):
        return {"bal": (bx % NX) * NZ + bz % NZ}

    def seq(sy, sc):
        return {"seq": (sy % NY) * 2 + sc}

    z_up, z_dn = bal(x, z + 1), bal(x, z + NZ - 1)
    x_up, x_dn = bal(x + 1, z), bal(x + NX - 1, z)
    y_up, y_dn = seq(y + 1, core), seq(y + NY - 1, core)
    other = seq(y, 1 - core)

    def move(src, dst, send, recv, where):
        return pltpu.make_async_remote_copy(
            src_ref=src, dst_ref=dst, send_sem=send, recv_sem=recv, device_id=where, device_id_type=MESH
        )

    started = []

    def go(ref, send, recv, where):
        c = move(ref, ref, send, recv, where)
        c.start()
        started.append(c)

    def arrived(ref, send, recv):
        move(ref, ref, send, recv, z_up).wait_recv()

    barrier = pltpu.get_barrier_semaphore()

    @pl.loop(1, N_BAL)
    def _(d):
        pl.semaphore_signal(barrier, inc=1, device_id={"bal": (me + d) % N_BAL}, device_id_type=MESH)

    @pl.loop(1, N_SEQ)
    def _(d):
        pl.semaphore_signal(barrier, inc=1, device_id={"seq": (sq + d) % N_SEQ}, device_id_type=MESH)

    for h in range(LOCAL_HEADS):
        wbuf[x, z, :, h * WIDTH : (h + 1) * WIDTH] = w_in[h]
    lane8 = lax.broadcasted_iota(jnp.int32, (8, 128), 1)
    owners_row = jnp.full((8, 128), -1, jnp.int32)
    for i in range(TILES_OWN):
        owners_row = jnp.where(lane8 == i, tile_owner[i], owners_row)
    row_own[...] = owners_row
    row_all[me] = owners_row

    ends, sizes = [], []
    total = 0
    for k in range(MAXCLIPS):
        f, h, w = (clip_dims[3 * k + i] for i in range(3))
        total = total + f * h * w
        ends.append(total)
        sizes.append((h, w))

    def clip_at(index):
        return sum((index >= ends[k]).astype(jnp.int32) for k in range(MAXCLIPS))

    def layout(index):
        member = clip_at(index)
        start, height, width = (jnp.zeros_like(index) for _ in range(3))
        for k in range(MAXCLIPS):
            here = member == k
            start = jnp.where(here, ends[k - 1] if k else 0, start)
            height = jnp.where(here, sizes[k][0], height)
            width = jnp.where(here, sizes[k][1], width)
        offset = index - start
        frame = (offset >= height * width).astype(jnp.int32)
        offset = offset - frame * height * width
        row = (offset >= width).astype(jnp.int32) + (offset >= 2 * width).astype(jnp.int32)
        return member, frame, row, offset - row * width

    upper = lax.broadcasted_iota(jnp.int32, (8, half_d), 0) < HALF

    def interleave(a, b):
        return jnp.where(upper, a, pltpu.roll(b, HALF, 0)), jnp.where(upper, pltpu.roll(a, HALF, 0), b)

    @pl.loop(0, TILES_OWN)
    def _(i):
        values = tok[i].astype(jnp.float32)
        for t, half in enumerate(interleave(values[:, :half_d], values[:, half_d:])):
            halves[t, i] = half.astype(jnp.bfloat16)

    def tables():
        of_query = layout(lax.broadcasted_iota(jnp.int32, (GROUP, GROUP), 0) % (GROUP // 2) // HALF)
        of_key = layout(lax.broadcasted_iota(jnp.int32, (GROUP, GROUP), 1) % (GROUP // 2) // HALF)
        allowed = of_query[0] == of_key[0]
        for a, b in zip(of_query[1:], of_key[1:], strict=True):
            allowed = allowed & (jnp.abs(a - b) <= 1)
        bias_tile = jnp.where(allowed, 0.0, score_fill)
        for s in range(N_SEQ):
            bias[:, s * GROUP : (s + 1) * GROUP] = bias_tile

        for k in range(MAXCLIPS):
            for which in range(2):
                line = mod[0, k, which : which + 1, :]
                mods[k, which] = jnp.where(upper, line[:, :half_d], line[:, half_d:]) + float(which)

    pl.semaphore_wait(barrier, N_BAL + N_SEQ - 2)

    def b_piece(bx, bz, lo=0, size=ROWS_B):
        return wbuf.at[bx % NX, bz % NZ, pl.ds(lo, size)]

    def a_piece(bx, bz, lo=0, size=rows - ROWS_B):
        return wbuf.at[bx % NX, bz % NZ, pl.ds(ROWS_B + lo, size)]

    def a_block(bz, lo=0, size=NX):
        return wbuf.at[pl.ds(lo, size), bz % NZ, pl.ds(ROWS_B, rows - ROWS_B)]

    def owner_row(d, to, slot):
        return move(row_own, row_all.at[slot], own_s.at[d], own_r.at[d], {"bal": to})

    def relay(t, d, to, slot):
        return move(obuf.at[t, to], rbuf[t].at[slot], rel_s.at[t, d], rel_r.at[t, d], {"bal": to})

    def back_relay(h, d, to, slot):
        return move(back.at[h, to], came_back[h].at[slot], ret_s.at[h, d], ret_r.at[h, d], {"bal": to})

    def send_x(j, bz):
        go(b_piece(x, bz), x_s.at[0, j], x_r.at[0, j], x_up)
        go(b_piece(x, bz), x_s.at[1, j], x_r.at[1, j], x_dn)

    def pass_x(j, bz):
        arrived(b_piece(x + NX - 1, bz), x_s.at[0, j], x_r.at[0, j])
        go(b_piece(x + NX - 1, bz, 0, half_b), xf_s.at[0, j], xf_r.at[0, j], x_up)
        arrived(b_piece(x + 1, bz), x_s.at[1, j], x_r.at[1, j])
        go(b_piece(x + 1, bz, half_b, half_b), xf_s.at[1, j], xf_r.at[1, j], x_dn)

    def tiles_out():
        def tile_for(owner):
            tile = 0
            for i in range(1, TILES_OWN):
                tile = jnp.where(tile_owner[i] == owner, i, tile)
            return tile

        mine = tile_for(me)
        for t in range(2):
            rbuf[t][me] = halves[t, mine]

        @pl.loop(1, N_BAL)
        def _(d):
            to = (me + d) % N_BAL
            owner_row(d, to, me).start()
            tile = tile_for(to)
            obuf[0, to] = halves[0, tile]
            relay(0, d, to, me).start()
            obuf[1, to] = halves[1, tile]

    def find_sources():
        @pl.loop(1, N_BAL)
        def _(d):
            source = (me + N_BAL - d) % N_BAL
            move(row_own, row_all.at[source], own_s.at[d], own_r.at[d], z_up).wait_recv()

        source_id = lax.broadcasted_iota(jnp.int32, (N_BAL, 128), 0)
        lane = lax.broadcasted_iota(jnp.int32, (N_BAL, 128), 1)
        hits = (row_all[:, 0, :] == me).astype(jnp.int32)
        gives = jnp.broadcast_to(jnp.max(hits, axis=1, keepdims=True), (N_BAL, 128))
        upto = gives
        for shift in (1, 2, 4, 8, 16):
            upto = upto + jnp.where(source_id >= shift, pltpu.roll(upto, shift, 0), 0)
        position = upto - gives
        found = jnp.where((gives > 0) & (position == lane), source_id, 0)
        place[0:N_BAL] = jnp.minimum(position, TILES_OWN - 1)
        place[N_BAL : N_BAL + 8] = jnp.broadcast_to(jnp.sum(found, axis=0, keepdims=True), (8, 128))
        fetch = pltpu.make_async_copy(place, place_s, place_sem)
        fetch.start()
        fetch.wait()

    def tiles_in(t):
        @pl.loop(1, N_BAL)
        def _(d):
            source = (me + N_BAL - d) % N_BAL
            move(obuf.at[t, source], rbuf[t].at[source], rel_s.at[t, d], rel_r.at[t, d], z_up).wait_recv()

        if t == 0:
            @pl.loop(1, N_BAL)
            def _(d):
                relay(1, d, (me + d) % N_BAL, me).start()

        def over_features(values):
            line = jnp.sum(values, axis=-1, keepdims=True)
            line = jnp.broadcast_to(line, (8, 128))
            return ((line + pltpu.roll(line, HALF, 0)) * (1.0 / d_model))[:, 0:1]

        def normed(r):
            values = rbuf[t][place_s[N_BAL, r]].astype(jnp.float32)
            away = values - over_features(values)
            spread = over_features(away * away)
            clip = jnp.minimum(clip_at(r), MAXCLIPS - 1)
            return away * lax.rsqrt(spread + eps_norm) * mods[clip, 1] + mods[clip, 0]

        @pl.loop(0, PAIRS)
        def _(p):
            low, high = interleave(normed(2 * p), normed(2 * p + 1))
            gbuf[sq, t, p, :, :half_d] = low.astype(jnp.bfloat16)
            gbuf[sq, t, p, :, half_d:] = high.astype(jnp.bfloat16)

        go(piece(t, y, core), y_s.at[0, t], y_r.at[0, t], y_up)
        go(piece(t, y, core), y_s.at[1, t], y_r.at[1, t], y_dn)
        go(piece(t, y, core), c_s.at[0, t], c_r.at[0, t], other)

    def step_z(k):
        if k < NZ // 2:
            size, lo = (ROWS_B, 0) if k < NZ // 2 - 1 else (half_b, half_b)
            arrived(b_piece(x, z + NZ - k), z_s.at[0, k], z_r.at[0, k])
            go(b_piece(x, z + NZ - k, 0, size), z_s.at[0, k + 1], z_r.at[0, k + 1], z_up)
            arrived(b_piece(x, z + k), z_s.at[1, k], z_r.at[1, k])
            go(b_piece(x, z + k, lo, size), z_s.at[1, k + 1], z_r.at[1, k + 1], z_dn)
            send_x(NZ - k, z + NZ - k)
            send_x(k, z + k)
        else:
            arrived(b_piece(x, z + k, 0, half_b), z_s.at[0, k], z_r.at[0, k])
            arrived(b_piece(x, z + k, half_b, half_b), z_s.at[1, k], z_r.at[1, k])
            send_x(k, z + k)

    def a_forward():
        arrived(a_piece(x + NX - 1, z), ax_s.at[0], ax_r.at[0])
        go(a_piece(x + NX - 1, z, 0, half_a), axf_s.at[0], axf_r.at[0], x_up)
        arrived(a_piece(x + 1, z), ax_s.at[1], ax_r.at[1])
        go(a_piece(x + 1, z, half_a, half_a), axf_s.at[1], axf_r.at[1], x_dn)

    def step_az(k):
        if k == 0:
            arrived(a_piece(x + 2, z, 0, half_a), axf_s.at[0], axf_r.at[0])
            arrived(a_piece(x + 2, z, half_a, half_a), axf_s.at[1], axf_r.at[1])
            go(a_block(z), az_s.at[0, 1], az_r.at[0, 1], z_up)
            go(a_block(z), az_s.at[1, 1], az_r.at[1, 1], z_dn)
        elif k < NZ // 2:
            size, lo = (NX, 0) if k < NZ // 2 - 1 else (NX // 2, NX // 2)
            arrived(a_block(z + NZ - k), az_s.at[0, k], az_r.at[0, k])
            go(a_block(z + NZ - k, 0, size), az_s.at[0, k + 1], az_r.at[0, k + 1], z_up)
            arrived(a_block(z + k), az_s.at[1, k], az_r.at[1, k])
            go(a_block(z + k, lo, size), az_s.at[1, k + 1], az_r.at[1, k + 1], z_dn)
        else:
            arrived(a_block(z + k, 0, NX // 2), az_s.at[0, k], az_r.at[0, k])
            arrived(a_block(z + k, NX // 2, NX // 2), az_s.at[1, k], az_r.at[1, k])

    def step_p(j):
        pass_x(j, z + j)
        if j not in (0, NZ // 2):
            pass_x(NZ - j, z + NZ - j)

    def far_x():
        for j in range(NZ):
            arrived(b_piece(x + 2, z + j, 0, half_b), xf_s.at[0, j], xf_r.at[0, j])
            arrived(b_piece(x + 2, z + j, half_b, half_b), xf_s.at[1, j], xf_r.at[1, j])

    half_p = PAIRS // 2

    def piece(t, sy, sc, lo=0, size=PAIRS):
        return gbuf.at[(sy % NY) * 2 + sc, t, pl.ds(lo, size)]

    def near_y(t):
        for way, (frm, to) in enumerate(((y + NY - 1, y_up), (y + 1, y_dn))):
            arrived(piece(t, frm, core), y_s.at[way, t], y_r.at[way, t])
            go(piece(t, frm, core, way * half_p, half_p), yf_s.at[way, t], yf_r.at[way, t], to)
            go(piece(t, frm, core), c_s.at[1 + way, t], c_r.at[1 + way, t], other)

    def far_y(t):
        for way in range(2):
            far = piece(t, y + 2, core, way * half_p, half_p)
            arrived(far, yf_s.at[way, t], yf_r.at[way, t])
            go(far, c_s.at[3 + way, t], c_r.at[3 + way, t], other)
        arrived(piece(t, y, 1 - core), c_s.at[0, t], c_r.at[0, t])
        for way, frm in enumerate((y + NY - 1, y + 1)):
            arrived(piece(t, frm, 1 - core), c_s.at[1 + way, t], c_r.at[1 + way, t])
            arrived(piece(t, y + 2, 1 - core, way * half_p, half_p), c_s.at[3 + way, t], c_r.at[3 + way, t])

    tokens_all = N_SEQ * GROUP

    def left(g):
        columns = pl.ds(pl.multiple_of(g * k_group, 128), k_group)
        return gbuf[:, :, :, :, columns].reshape(tokens_all, k_group)

    def project_qk(g, first):
        @pl.loop(0, LOCAL_HEADS)
        def _(h):
            cols = pl.ds(pl.multiple_of(h * WIDTH, HD), 2 * HD)
            right = wbuf[g, :, :, cols].reshape(k_group, 2 * HD)
            product = jnp.dot(left(g), right, preferred_element_type=jnp.float32)
            if first:
                acc[:, cols] = product
            else:
                acc[:, cols] += product

    def project_v(g, first):
        right = jnp.concatenate(
            [wbuf[g, :, :, h * WIDTH + 2 * HD : (h + 1) * WIDTH].reshape(k_group, HD) for h in range(LOCAL_HEADS)],
            axis=1,
        )
        product = jnp.dot(left(g), right, preferred_element_type=jnp.float32)
        for h in range(LOCAL_HEADS):
            cols = slice(h * WIDTH + 2 * HD, (h + 1) * WIDTH)
            if first:
                acc[:, cols] = product[:, h * HD : (h + 1) * HD]
            else:
                acc[:, cols] += product[:, h * HD : (h + 1) * HD]

    def project_near():
        for i, step in enumerate((0, 1, NX - 1)):
            project_qk((x + step) % NX, i == 0)

    go(b_piece(x, z), z_s.at[0, 1], z_r.at[0, 1], z_up)
    go(b_piece(x, z), z_s.at[1, 1], z_r.at[1, 1], z_dn)
    go(a_piece(x, z), ax_s.at[0], ax_r.at[0], x_up)
    go(a_piece(x, z), ax_s.at[1], ax_r.at[1], x_dn)
    for event in ORDER:
        if event == "R0":
            tiles_out()
            tables()
        elif event == "R1":
            find_sources()
            tiles_in(0)
        elif event == "R2":
            tiles_in(1)
        elif event == "X0":
            send_x(0, z)
        elif event == "AF":
            a_forward()
        elif event == "F":
            far_x()
        elif event == "M1":
            project_near()
        elif event == "M2":
            project_qk((x + 2) % NX, False)
        else:
            number = int(event[1])
            if event[0] == "Y":
                near_y(number - 1)
            elif event[0] == "F":
                far_y(number - 1)
            else:
                {"A": step_az, "Z": step_z, "P": step_p}[event[0]](number)

    @pl.loop(0, N_SEQ)
    def _(s):
        lines = pl.ds(pl.multiple_of(s * GROUP, GROUP), GROUP)
        for which in range(2):
            squares = sum(
                jnp.square(acc[lines, h * WIDTH + which * HD : h * WIDTH + (which + 1) * HD])
                for h in range(LOCAL_HEADS)
            )
            line = jnp.sum(squares.T, axis=0, keepdims=True)
            sums[sq, which * 8 : which * 8 + 8, lines] = jnp.broadcast_to(line, (8, GROUP))

    def sum_row(d, to, slot):
        return move(sums.at[sq], sums.at[slot], sum_s.at[d], sum_r.at[d], {"seq": to})

    for d in range(1, N_SEQ):
        sum_row(d, (sq + d) % N_SEQ, sq).start()
    for i, step in enumerate((0, 1, NX - 1, 2)):
        project_v((x + step) % NX, i == 0)

    for d in range(1, N_SEQ):
        source = (sq + N_SEQ - d) % N_SEQ
        move(sums.at[source], sums.at[source], sum_s.at[d], sum_r.at[d], z_up).wait_recv()

    @pl.loop(0, N_SEQ)
    def _(s):
        lines = pl.ds(pl.multiple_of(s * GROUP, GROUP), GROUP)
        for which, gain, to in ((0, q_gain, qn), (1, k_gain, kn)):
            line = sum(sums[t, which * 8 : which * 8 + 8, lines] for t in range(N_SEQ))
            scale = lax.rsqrt(line / (HEADS * HD) + eps_norm)
            scale = jnp.broadcast_to(scale[0:1], (HD, GROUP)).T
            for h in range(LOCAL_HEADS):
                raw = acc[lines, h * WIDTH + which * HD : h * WIDTH + (which + 1) * HD]
                to[h, lines] = (raw * scale * gain[h : h + 1]).astype(jnp.bfloat16)
        for h in range(LOCAL_HEADS):
            vn[h, lines] = acc[lines, h * WIDTH + 2 * HD : (h + 1) * WIDTH].astype(jnp.bfloat16)

    def attend(h, s):
        lines = pl.ds(pl.multiple_of(s * GROUP, GROUP), GROUP)
        scores = lax.dot_general(
            qn[h, lines], kn[h], (((1,), (1,)), ((), ())), preferred_element_type=jnp.float32
        )
        scores = scores * (HD**-0.5 * LOG2_E) + bias[...]
        weights = jnp.exp2(scores - jnp.max(scores, axis=-1, keepdims=True))
        totals = jnp.sum(weights, axis=-1, keepdims=True)
        result = jnp.dot(
            weights.astype(jnp.bfloat16), vn[h], preferred_element_type=jnp.float32
        ) / totals
        result = result.reshape(2, PAIRS, 8, HD)
        first, second = result[0], result[1]
        top = lax.broadcasted_iota(jnp.int32, (PAIRS, 8, HD), 1) < HALF
        even = jnp.where(top, first, pltpu.roll(second, HALF, 1))
        odd = jnp.where(top, pltpu.roll(first, HALF, 1), second)
        return jnp.stack([even, odd], axis=1).reshape(TILES_OWN, PER, HD).astype(jnp.bfloat16)

    def head_group(h, d, to, slot):
        return move(att.at[h, to], heads[h].at[slot], att_s.at[h, d], att_r.at[h, d], {"seq": to})

    def attend_all(h):
        @pl.loop(1, N_SEQ)
        def _(d):
            to = (sq + d) % N_SEQ
            att[h, to] = attend(h, to)
            head_group(h, d, to, sq).start()

        heads[h][sq] = attend(h, sq)

    def send_back(h):
        @pl.loop(1, N_SEQ)
        def _(d):
            source = (sq + N_SEQ - d) % N_SEQ
            move(att.at[h, source], heads[h].at[source], att_s.at[h, d], att_r.at[h, d], z_up).wait_recv()

        @pl.loop(1, N_BAL)
        def _(d):
            to = (me + d) % N_BAL
            tile = place_s[to, 0]
            for s in range(N_SEQ):
                back[h, to, :, s * HD : (s + 1) * HD] = heads[h][s, tile]
            back_relay(h, d, to, me).start()

        tile = place_s[me, 0]
        for s in range(N_SEQ):
            came_back[h][me, :, s * HD : (s + 1) * HD] = heads[h][s, tile]

    for h in range(LOCAL_HEADS):
        attend_all(h)
        if h:
            send_back(h - 1)
    send_back(LOCAL_HEADS - 1)

    for h in range(LOCAL_HEADS):
        @pl.loop(1, N_BAL)
        def _(d, h=h):
            source = (me + N_BAL - d) % N_BAL
            move(back.at[h, source], came_back[h].at[source], ret_s.at[h, d], ret_r.at[h, d], z_up).wait_recv()

        for i in range(TILES_OWN):
            tile = came_back[h][tile_owner[i]]
            for s in range(N_SEQ):
                column = (s * LOCAL_HEADS + h) * HD
                out[i, :, column : column + HD] = tile[:, s * HD : (s + 1) * HD]

    @pl.loop(1, N_BAL)
    def _(d):
        to = (me + d) % N_BAL
        owner_row(d, to, me).wait_send()
        relay(0, d, to, me).wait_send()
        relay(1, d, to, me).wait_send()
        for h in range(LOCAL_HEADS):
            back_relay(h, d, to, me).wait_send()

    @pl.loop(1, N_SEQ)
    def _(d):
        to = (sq + d) % N_SEQ
        sum_row(d, to, sq).wait_send()
        for h in range(LOCAL_HEADS):
            head_group(h, d, to, sq).wait_send()

    for c in started:
        c.wait_send()


def per_device(tokens, w_qkv, q_gain, k_gain, modulation, tile_owner, clip_dims):
    tiles, per, d_model = tokens.shape
    rows = w_qkv.shape[0]
    dma = pltpu.SemaphoreType.DMA
    vmem = pl.BlockSpec(memory_space=pltpu.VMEM)
    smem = pl.BlockSpec(memory_space=pltpu.SMEM)
    m = N_SEQ * GROUP
    columns = LOCAL_HEADS * WIDTH
    bf16, f32, i32 = jnp.bfloat16, jnp.float32, jnp.int32
    call = pl.pallas_call(
        kernel,
        out_shape=jax.ShapeDtypeStruct((tiles, per, HEADS * HD), bf16),
        in_specs=[smem] * 2 + [vmem] * 5,
        out_specs=vmem,
        scratch_shapes=[
            pltpu.VMEM((NX, NZ, rows, columns), bf16),
            pltpu.VMEM((N_SEQ, 2, PAIRS, 8, d_model), bf16),
            pltpu.VMEM((2, tiles, 8, d_model // 2), bf16),
            pltpu.VMEM((MAXCLIPS, 2, 8, d_model // 2), f32),
            pltpu.VMEM((2, N_BAL, 8, d_model // 2), bf16),
            pltpu.VMEM((N_BAL, 8, d_model // 2), bf16),
            pltpu.VMEM((N_BAL, 8, d_model // 2), bf16),
            pltpu.VMEM((m, columns), f32),
            pltpu.VMEM((8, 128), i32),
            pltpu.VMEM((N_BAL, 8, 128), i32),
            pltpu.VMEM((N_BAL + 8, 128), i32),
            pltpu.VMEM((N_SEQ, 16, m), f32),
            pltpu.VMEM((GROUP, m), f32),
            pltpu.VMEM((LOCAL_HEADS, m, HD), bf16),
            pltpu.VMEM((LOCAL_HEADS, m, HD), bf16),
            pltpu.VMEM((LOCAL_HEADS, m, HD), bf16),
            pltpu.VMEM((LOCAL_HEADS, N_SEQ, tiles, per, HD), bf16),
            *[pltpu.VMEM((N_SEQ, tiles, per, HD), bf16)] * LOCAL_HEADS,
            pltpu.VMEM((LOCAL_HEADS, N_BAL, per, N_SEQ * HD), bf16),
            *[pltpu.VMEM((N_BAL, per, N_SEQ * HD), bf16)] * LOCAL_HEADS,
            pltpu.SMEM((N_BAL + 8, 128), i32),
            dma((2, N_BAL)), dma((2, N_BAL)),
            dma((2, 5)), dma((2, 5)),
            dma((2, NZ)), dma((2, NZ)),
            dma((2, NZ)), dma((2, NZ)),
            dma((2,)), dma((2,)), dma((2,)), dma((2,)),
            dma((2, 5)), dma((2, 5)),
            dma((2, 2)), dma((2, 2)), dma((2, 2)), dma((2, 2)),
            dma((5, 2)), dma((5, 2)),
            dma((N_BAL,)), dma((N_BAL,)), dma,
            dma((N_SEQ,)), dma((N_SEQ,)),
            dma((LOCAL_HEADS, N_SEQ)), dma((LOCAL_HEADS, N_SEQ)),
            dma((LOCAL_HEADS, N_BAL)), dma((LOCAL_HEADS, N_BAL)),
        ],
        compiler_params=pltpu.CompilerParams(
            collective_id=0, has_side_effects=True, vmem_limit_bytes=58 * 2**20
        ),
        cost_estimate=pl.CostEstimate(
            flops=2 * m * d_model * columns, bytes_accessed=8 * 2**20, transcendentals=0
        ),
        name="relaid_tile_attention",
    )
    return call(
        tile_owner, clip_dims.reshape(-1), tokens, w_qkv.transpose(1, 0, 2), modulation, q_gain, k_gain
    )


def solution(mesh):
    return jax.shard_map(
        per_device,
        mesh=mesh,
        in_specs=(
            P("bal", "seq", None),
            P("bal", "seq", None),
            P("seq", None),
            P("seq", None),
            P("bal", None, None, None),
            P("bal"),
            P("bal", None, None),
        ),
        out_specs=P("bal", "seq", None),
        check_vma=False,
    )
```
